32 devices in a mesh: row: 4 (over y, x), col: 8 (over z, core).
Axes of the slice: x: 2, y: 2, z: 4, core: 2. Of those that a mesh axis runs over, the one named last changes fastest.
Arguments:
- div_blocks: float32 [64, 6, 128, 128], P(('row', 'col')), may hold values from -0.5 to 0.5
- div_owner: int32 [64, 6], P(('row', 'col')), may hold values from 0 to 3, as said below
- div_local: int32 [64, 6], P(('row', 'col')), may hold values from 0 to 1
- div_count: int32 [64], P(('row', 'col')), may hold values from 2 to 6
- inv_blocks: float32 [64, 5, 128, 128], P(('row', 'col')), may hold values from -6 to 6
- inv_cols: int32 [64, 5], P(('row', 'col')), may hold values from 0 to 5, as said below
- inv_count: int32 [64], P(('row', 'col')), may hold values from 3 to 5
- schur_cols: int32 [64, 4], P(('row', 'col')), may hold values from 0 to 63, as said below
- schur_count: int32 [64], P(('row', 'col')), may hold values from 2 to 4
Outputs:
- schur_blocks: float32 [64, 4, 128, 128], P(('row', 'col'))
The draws below stay inside these ranges and needn't reach their ends.
Inputs may be any that keep to these rules, and one draw needn't show every extreme that they name: `div_owner`: over all 6 slots of the 2 rows of one device, live or not, at most 3 name the same owner, and exactly 3 do for some owner on every device. `inv_cols`: the columns of one row are distinct. `schur_cols`: slot 0 of row p is p itself, slot 1 another row of the same subdomain, slot 2 a row of the subdomain with the same a and c + 1 mod 8, slot 3 one of the subdomain with c - 1 mod 8.
All inputs are finite; a program needn't handle non-finite values.
Results may differ from the reference program's by a relative error of at most 0.0003.
Values sent between devices are 32-bit elements; how exact they have to be, the bound alone decides.
No kernel may reach another device: no remote copies, remote signals or barrier semaphores. Data moves between devices by JAX's collectives and lax.ppermute only.
A program may use at most 128 MiB of HBM per device.

```python
import jax
import jax.numpy as jnp
from jax import lax

BS = 128
PB_DEV = 2
VB_DEV = 2
KB = 6
KM = 5
KS = 4
OWNERS = 4
LONGITUDES = 8
CAP = 3
NP = 64
NV = 64


def draw_div_owner(key, part):
    groups = NP // PB_DEV
    listed = PB_DEV * KB
    first_key, second_key = jax.random.split(jax.random.fold_in(key, 11))
    owner_base = jnp.tile(jnp.arange(OWNERS, dtype=jnp.int32)[None, :], (groups, 1))
    owner_order = jax.random.permutation(first_key, owner_base, axis=1, independent=True)
    picks = jnp.arange(listed, dtype=jnp.int32) // CAP
    sequence = owner_order[:, picks]
    spot_base = jnp.tile(jnp.arange(listed, dtype=jnp.int32)[None, :], (groups, 1))
    spot_order = jax.random.permutation(second_key, spot_base, axis=1, independent=True)
    owners_drawn = jnp.take_along_axis(sequence, spot_order, axis=1)
    return owners_drawn.reshape(NP, KB)


def draw_inv_cols(key, part):
    column_base = jnp.tile(jnp.arange(3 * VB_DEV, dtype=jnp.int32)[None, :], (NV, 1))
    column_order = jax.random.permutation(jax.random.fold_in(key, 17), column_base, axis=1, independent=True)
    return column_order[:, :KM]


def draw_schur_cols(key, part):
    first_key, second_key, third_key = jax.random.split(jax.random.fold_in(key, 23), 3)
    row_ids = jnp.arange(NP, dtype=jnp.int32)
    device_ids = row_ids // PB_DEV
    local_ids = row_ids % PB_DEV
    slab_ids = device_ids // LONGITUDES
    lon_ids = device_ids % LONGITUDES
    step_other = jax.random.randint(first_key, (NP,), 1, PB_DEV, dtype=jnp.int32)
    other_row = device_ids * PB_DEV + (local_ids + step_other) % PB_DEV
    right_row = (slab_ids * LONGITUDES + (lon_ids + 1) % LONGITUDES) * PB_DEV + jax.random.randint(second_key, (NP,), 0, PB_DEV, dtype=jnp.int32)
    left_row = (slab_ids * LONGITUDES + (lon_ids + LONGITUDES - 1) % LONGITUDES) * PB_DEV + jax.random.randint(third_key, (NP,), 0, PB_DEV, dtype=jnp.int32)
    return jnp.stack([row_ids, other_row, right_row, left_row], axis=1)


def plant(result, rng, least, largest):
    longest = result.shape.index(max(result.shape))
    spots = []
    for shift in (0, 1):
        where = [jax.random.randint(jax.random.fold_in(rng, axis), (), 0, length) for axis, length in enumerate(result.shape)]
        where[longest] = (where[longest] + shift) % result.shape[longest]
        spots.append(tuple(where))
    return result.at[spots[0]].set(least).at[spots[1]].set(largest)


def level_of(rng, shape, cuts, least, top_value):
    def one(axis_at, shards_of):
        heights = jax.random.uniform(jax.random.fold_in(jax.random.fold_in(rng, 6), axis_at), (shards_of,), jnp.float32, least / len(cuts), top_value / len(cuts))
        return jnp.repeat(jnp.exp(heights), shape[axis_at] // shards_of).reshape((-1,) + (1,) * (len(shape) - axis_at - 1))

    gain = one(*cuts[0])
    for cut in cuts[1:]:
        gain = gain * one(*cut)
    return gain


def noise(key, shape, deviation, most, shards=(), kind=jnp.bfloat16):
    level = level_of(key, shape, shards, -0.22, 0.18) if shards else 1.0
    drawn = jax.random.normal(key, shape, jnp.float32) * deviation * level
    return jnp.minimum(jnp.maximum(drawn, -most), most).astype(kind)


def setup_inputs(seed: int = 0) -> dict:
    splits = jax.random.split(jax.random.key(seed), 10)
    return {
        "div_blocks": noise(splits[0], (NP, KB, BS, BS), BS ** -0.5, 0.5, ((0, 32),), jnp.float32),
        "div_owner": draw_div_owner(jax.random.fold_in(splits[9], 71), 0),
        "div_local": plant(jax.random.randint(splits[2], (NP, KB), 0, VB_DEV), jax.random.fold_in(splits[2], 1), 0, VB_DEV - 1).astype(jnp.int32),
        "div_count": plant(jax.random.randint(splits[3], (NP,), 2, KB + 1), jax.random.fold_in(splits[3], 1), 2, KB).astype(jnp.int32),
        "inv_blocks": noise(splits[4], (NV, KM, BS, BS), 1.0, 6.0, ((0, 32),), jnp.float32),
        "inv_cols": draw_inv_cols(jax.random.fold_in(splits[9], 71), 0),
        "inv_count": plant(jax.random.randint(splits[6], (NV,), 3, KM + 1), jax.random.fold_in(splits[6], 1), 3, KM).astype(jnp.int32),
        "schur_cols": draw_schur_cols(jax.random.fold_in(splits[9], 71), 0),
        "schur_count": plant(jax.random.randint(splits[8], (NP,), 2, KS + 1), jax.random.fold_in(splits[8], 1), 2, KS).astype(jnp.int32),
    }


def reference(div_blocks, div_owner, div_local, div_count, inv_blocks, inv_cols, inv_count, schur_cols, schur_count):
    press_ids = jnp.arange(NP, dtype=jnp.int32)
    lon_index = (press_ids // PB_DEV) % LONGITUDES
    vel_ids = (div_owner * LONGITUDES + lon_index[:, None]) * VB_DEV + div_local
    slot_live = jnp.arange(KB, dtype=jnp.int32)[None, :] < div_count[:, None]
    vel_rows = jnp.arange(NV, dtype=jnp.int32)
    vel_dev = vel_rows // VB_DEV
    slab_index = vel_dev // LONGITUDES
    vel_lon = vel_dev % LONGITUDES
    shifted = (vel_lon[:, None] + inv_cols // VB_DEV - 1 + LONGITUDES) % LONGITUDES
    inv_ids = (slab_index[:, None] * LONGITUDES + shifted) * VB_DEV + inv_cols % VB_DEV
    inv_live = jnp.arange(KM, dtype=jnp.int32)[None, :] < inv_count[:, None]
    pattern_live = jnp.arange(KS, dtype=jnp.int32)[None, :] < schur_count[:, None]

    def one_row(row):
        row_blocks = div_blocks[row]
        vel_here = vel_ids[row]
        live_here = slot_live[row]
        inv_rows = inv_blocks[vel_here]
        inv_here = inv_ids[vel_here]
        inv_ok = inv_live[vel_here] & live_here[:, None]
        partial_value = jnp.einsum("kpq,kmqr->kmpr", row_blocks, inv_rows, precision=lax.Precision.HIGHEST)
        others = schur_cols[row]
        other_ids = vel_ids[others]
        other_live = slot_live[others] & pattern_live[row][:, None]
        matches = (inv_here[None, :, :, None] == other_ids[:, None, None, :]) & inv_ok[None, :, :, None] & other_live[:, None, None, :]
        summed = jnp.einsum("tkml,kmpr->tlpr", matches.astype(jnp.float32), partial_value, precision=lax.Precision.HIGHEST)
        return jnp.einsum("tlpr,tlsr->tps", summed, div_blocks[others], precision=lax.Precision.HIGHEST)

    return lax.map(one_row, press_ids)
```

```python
import functools

import jax
import jax.numpy as jnp
from jax import lax
from jax.experimental import pallas as pl
from jax.experimental.pallas import tpu as pltpu
from jax.sharding import PartitionSpec as P

F32 = jnp.float32
BF16 = jnp.bfloat16
VMEM = pl.BlockSpec(memory_space=pltpu.VMEM)
SMEM = pl.BlockSpec(memory_space=pltpu.SMEM)
HALO, TARGETS = 32, 64


def halves(value):
    high = value.astype(BF16)
    return high, (value - high.astype(F32)).astype(BF16)


def product(left, right, transposed=False):
    dims = (((1,), (1 if transposed else 0,)), ((), ()))
    dot = functools.partial(lax.dot_general, dimension_numbers=dims, preferred_element_type=F32)
    return dot(left[0], right[0]) + (dot(left[0], right[1]) + dot(left[1], right[0]))


def clear(ref):
    ref[...] = jnp.zeros(ref.shape, ref.dtype)


def place_div(codes, blocks, sizes, dense):
    rows, slots, _, _, side = sizes
    for row in range(rows):
        for slot in range(slots):
            code = codes[row * slots + slot]

            @pl.when(code >= 0)
            def _():
                dense[code, pl.ds(row * side, side), :] += blocks[pl.ds((row * slots + slot) * side, side), :]


def place_inv(codes, blocks, sizes, high, low, first=0):
    _, _, width, slots, side = sizes
    for row in range(width):
        for slot in range(slots):
            code = codes[first + row * slots + slot]

            @pl.when(code >= 0)
            def _():
                spot = (pl.ds(row * side, side), pl.ds(pl.multiple_of(code * side, side), side))
                high[spot], low[spot] = halves(blocks[pl.ds((row * slots + slot) * side, side), :])


def owner_part(dense, owner, width):
    return halves(jnp.concatenate([dense[owner * width + i] for i in range(width)], axis=1))


def write(out, region_sums, meta):
    rows, pattern, side, _ = out.shape
    for row in range(rows):
        for slot in range(pattern):
            code = meta[row * pattern + slot]
            values = region_sums[(1, 1, 2, 0)[slot]][row * side : (row + 1) * side, :]
            result = jnp.zeros((side, side), F32)
            for other in range(rows):
                result = jnp.where(code == other, values[:, other * side : (other + 1) * side], result)
            out[row, slot] = result


def kernel_pack(row_axis, div, inv, owner, velocity, d_count, cols, m_count, targets, s_count, d_out, m_out, *scratch):
    tables, (m_sem, d_sem, sems) = scratch[:-3], scratch[-3:]
    d_rows, m_rows = div.shape[0], inv.shape[0]
    big = [
        pltpu.make_async_copy(inv, m_out.at[pl.ds(0, m_rows)], m_sem),
        pltpu.make_async_copy(div, d_out.at[pl.ds(0, d_rows)], d_sem),
    ]
    small = [
        pltpu.make_async_copy(source, table, sems.at[i])
        for i, (source, table) in enumerate(zip((owner, velocity, d_count, cols, m_count, targets, s_count), tables))
    ]
    for copy in big + small:
        copy.start()
    for copy in small:
        copy.wait()
    owner, velocity, d_count, cols, m_count, targets, s_count = tables
    row, col = (lax.axis_index(name) for name in row_axis)
    rows, slots = owner.shape
    width, inv_slots = cols.shape
    pattern = targets.shape[1]
    lane = lax.broadcasted_iota(jnp.int32, (8, 128), 1)

    def tile(codes):
        values = jnp.full((8, 128), -1, jnp.int32)
        for spot, code in codes:
            values = jnp.where(lane == spot, code, values)
        return values.astype(F32)

    codes = []
    for i in range(rows):
        for k in range(slots):
            apart = owner[i, k] ^ row
            swapped = ((apart & 1) << 1) | (apart >> 1)
            live = k < d_count[i]
            even, odd = (jnp.where(live, x * width + velocity[i, k], -1) for x in (apart, swapped))
            here = jnp.where(col % 2 == 0, even, odd)
            there = jnp.where(col % 2 == 0, odd, even)
            codes += [(i * slots + k, here), (HALO + i * slots + k, there)]
        for t in range(pattern):
            codes.append((TARGETS + i * pattern + t, jnp.where(t < s_count[i], targets[i, t] % rows, -1)))
    d_out[pl.ds(d_rows, 8), :] = tile(codes)
    m_out[pl.ds(m_rows, 8), :] = tile(
        (u * inv_slots + m, jnp.where(m < m_count[u], cols[u, m], -1)) for u in range(width) for m in range(inv_slots)
    )
    for copy in big:
        copy.wait()


def integers(packed, table, sem):
    copy = pltpu.make_async_copy(packed.at[pl.ds(packed.shape[0] - 8, 8)], table, sem)
    copy.start()
    return copy


class Row:
    def __init__(self, table, first=0):
        self.table, self.first = table, first

    def __getitem__(self, i):
        return self.table[0, self.first + i].astype(jnp.int32)


def kernel_own(sizes, div, inv, b_high, b_low, y_high, y_low, s_own, dense, m_high, m_low, d_table, m_table, sems):
    rows, slots, width, inv_slots, side = sizes
    copies = [integers(div, d_table, sems.at[0]), integers(inv, m_table, sems.at[1])]
    clear(dense)
    clear(m_high)
    clear(m_low)
    for copy in copies:
        copy.wait()
    place_div(Row(d_table), div, sizes, dense)
    for owner in range(dense.shape[0] // width):
        b_high[owner], b_low[owner] = owner_part(dense, owner, width)
    place_inv(Row(m_table), inv, sizes, m_high, m_low)
    own = (b_high[0], b_low[0])
    y_high[...], y_low[...] = halves(product(own, (m_high[...], m_low[...])))
    size = own[0].shape[1]
    s_own[...] = product((y_high[:, size : 2 * size], y_low[:, size : 2 * size]), own, True)


def kernel_side(which, sizes, inv, b_high, b_low, s_in, y_high, y_low, s_out, m_high, m_low, m_table, sem):
    copy = integers(inv, m_table, sem)
    clear(m_high)
    clear(m_low)
    copy.wait()
    place_inv(Row(m_table), inv, sizes, m_high, m_low)
    part = (b_high[which], b_low[which])
    y_high[...], y_low[...] = halves(product(part, (m_high[...], m_low[...])))
    size = part[0].shape[1]
    s_out[...] = s_in[...] + product((y_high[:, size : 2 * size], y_low[:, size : 2 * size]), part, True)


def kernel_halo(sizes, prev, follow, *refs):
    ys, (s_prev, s_next, p_high, p_low, n_high, n_low, dense, p_table, n_table, sems) = refs[:6], refs[6:]
    width = sizes[2]
    size = p_high.shape[1]
    copies = [integers(prev, p_table, sems.at[0]), integers(follow, n_table, sems.at[1])]
    clear(dense)
    for copy in copies:
        copy.wait()
    place_div(Row(p_table, HALO), prev, sizes, dense.at[0])
    place_div(Row(n_table, HALO), follow, sizes, dense.at[1])
    for i, (total, high, low, start) in enumerate(((s_prev, p_high, p_low, 0), (s_next, n_high, n_low, 2 * size))):
        for owner in range(3):
            part = owner_part(dense.at[i], owner, width)
            left = (ys[2 * owner][:, start : start + size], ys[2 * owner + 1][:, start : start + size])
            term = product(left, part, True)
            total[...] = term if owner == 0 else total[...] + term
        high[...], low[...] = owner_part(dense.at[i], 3, width)


def kernel_last(sizes, inv, div, b_high, b_low, p_high, p_low, n_high, n_low, s_own, s_prev, s_next, out, *scratch):
    m_high, m_low, m_table, d_table, sems = scratch
    copies = [integers(inv, m_table, sems.at[0]), integers(div, d_table, sems.at[1])]
    clear(m_high)
    clear(m_low)
    for copy in copies:
        copy.wait()
    place_inv(Row(m_table), inv, sizes, m_high, m_low)
    own = (b_high[3], b_low[3])
    y_high, y_low = halves(product(own, (m_high[...], m_low[...])))
    size = own[0].shape[1]
    sums = []
    for region, (part, total) in enumerate(
        (((p_high[...], p_low[...]), s_prev), (own, s_own), ((n_high[...], n_low[...]), s_next))
    ):
        cut = slice(region * size, (region + 1) * size)
        sums.append(total[...] + product((y_high[:, cut], y_low[:, cut]), part, True))
    write(out, sums, Row(d_table, TARGETS))


def kernel_all(sizes, d_meta, p_meta, n_meta, m_meta, s_meta, div, prev, follow, inv, out, dense, sums, m_high, m_low):
    _, _, width, slots, _ = sizes
    clear(dense)
    clear(sums)
    for region, (meta, blocks) in enumerate(((p_meta, prev), (d_meta, div), (n_meta, follow))):
        place_div(meta, blocks, sizes, dense.at[region])

    @pl.loop(0, inv.shape[0])
    def _(owner):
        clear(m_high)
        clear(m_low)
        place_inv(m_meta, inv.at[owner], sizes, m_high, m_low, owner * width * slots)
        size = m_high.shape[0]
        own = owner_part(dense.at[1], owner, width)
        y_high, y_low = halves(product(own, (m_high[...], m_low[...])))
        for region in range(3):
            cut = slice(region * size, (region + 1) * size)
            sums[region] += product((y_high[:, cut], y_low[:, cut]), owner_part(dense.at[region], owner, width), True)

    write(out, [sums[region] for region in range(3)], s_meta)


def call(kernel, operands, outs, scratch, flops, scalars=0, specs=None, limit=24 << 20):
    moved = sum(x.size * x.dtype.itemsize for x in operands[scalars:] + outs)
    return pl.pallas_call(
        kernel,
        out_shape=outs if len(outs) > 1 else outs[0],
        in_specs=specs or [SMEM] * scalars + [VMEM] * (len(operands) - scalars),
        out_specs=[VMEM] * len(outs) if len(outs) > 1 else VMEM,
        scratch_shapes=scratch,
        compiler_params=pltpu.CompilerParams(vmem_limit_bytes=limit),
        cost_estimate=pl.CostEstimate(flops=flops, bytes_accessed=moved, transcendentals=0),
    )(*operands)


def local(div_blocks, div_owner, div_local, div_count, inv_blocks, inv_cols, inv_count, schur_cols, schur_count):
    rows, slots, side, _ = div_blocks.shape
    width, inv_slots = inv_cols.shape
    pattern = schur_cols.shape[1]
    owners = lax.axis_size("row")
    count = lax.axis_size("col")
    size, wide = width * side, 3 * width * side
    sizes = (rows, slots, width, inv_slots, side)
    forward = [(i, (i + 1) % count) for i in range(count)]
    backward = [(i, (i - 1) % count) for i in range(count)]
    div_flat = div_blocks.reshape(rows * slots * side, side)
    inv_flat = inv_blocks.reshape(width * inv_slots * side, side)

    square = jax.ShapeDtypeStruct((rows * side, rows * side), F32)
    half = jax.ShapeDtypeStruct((rows * side, size), BF16)
    every = jax.ShapeDtypeStruct((owners, rows * side, size), BF16)
    y_half = jax.ShapeDtypeStruct((rows * side, wide), BF16)
    result = jax.ShapeDtypeStruct((rows, pattern, side, side), F32)
    m_half = pltpu.VMEM((size, wide), BF16)
    one = 2 * 3 * rows * side * size * wide

    if owners != 4 or count % 2 or side != 128:

        def order(length):
            return jnp.arange(length, dtype=jnp.int32)[None, :]

        d_meta = jnp.where(order(slots) < div_count[:, None], div_owner * width + div_local, -1).reshape(-1)
        m_meta = jnp.where(order(inv_slots) < inv_count[:, None], inv_cols, -1).reshape(-1)
        s_meta = jnp.where(order(pattern) < schur_count[:, None], schur_cols % rows, -1).reshape(-1)
        prev = lax.ppermute(div_flat, "col", forward)
        follow = lax.ppermute(div_flat, "col", backward)
        p_meta = lax.ppermute(d_meta, "col", forward)
        n_meta = lax.ppermute(d_meta, "col", backward)
        inv = lax.all_gather(inv_flat, "row")
        all_meta = lax.all_gather(m_meta, "row", tiled=True)
        return call(
            functools.partial(kernel_all, sizes),
            [d_meta, p_meta, n_meta, all_meta, s_meta, div_flat, prev, follow, inv],
            [result],
            [
                pltpu.VMEM((3, owners * width, rows * side, side), F32),
                pltpu.VMEM((3, rows * side, rows * side), F32),
                m_half,
                m_half,
            ],
            owners * one * 2,
            scalars=5,
            limit=56 << 20,
        )

    def swap(first):
        def partner(r, c):
            return r ^ (1 if (c % 2 == 0) == first else 2)

        return [(r * count + c, partner(r, c) * count + c) for r in range(owners) for c in range(count)]

    table = pltpu.SMEM((8, 128), F32)
    tables = (div_owner, div_local, div_count, inv_cols, inv_count, schur_cols, schur_count)
    div, inv = call(
        functools.partial(kernel_pack, ("row", "col")),
        [div_flat, inv_flat, *tables],
        [jax.ShapeDtypeStruct((x.shape[0] + 8, side), F32) for x in (div_flat, inv_flat)],
        [pltpu.SMEM(x.shape, x.dtype) for x in tables]
        + [pltpu.SemaphoreType.DMA, pltpu.SemaphoreType.DMA, pltpu.SemaphoreType.DMA((len(tables),))],
        0,
        specs=[pl.BlockSpec(memory_space=pl.ANY)] * (2 + len(tables)),
        limit=60 << 20,
    )
    inv_1 = lax.ppermute(inv, ("row", "col"), swap(True))
    inv_2 = lax.ppermute(inv, ("row", "col"), swap(False))
    prev = lax.ppermute(div, "col", forward)
    follow = lax.ppermute(div, "col", backward)
    inv_3 = lax.ppermute(inv_1, ("row", "col"), swap(False))

    pair = pltpu.SemaphoreType.DMA((2,))
    b_high, b_low, y0_high, y0_low, s_own = call(
        functools.partial(kernel_own, sizes),
        [div, inv],
        [every, every, y_half, y_half, square],
        [pltpu.VMEM((owners * width, rows * side, side), F32), m_half, m_half, table, table, pair],
        one * 4 // 3,
    )
    y1_high, y1_low, s_own = call(
        functools.partial(kernel_side, 1, sizes),
        [inv_1, b_high, b_low, s_own],
        [y_half, y_half, square],
        [m_half, m_half, table, pltpu.SemaphoreType.DMA],
        one * 4 // 3,
    )
    y2_high, y2_low, s_own = call(
        functools.partial(kernel_side, 2, sizes),
        [inv_2, b_high, b_low, s_own],
        [y_half, y_half, square],
        [m_half, m_half, table, pltpu.SemaphoreType.DMA],
        one * 4 // 3,
    )
    s_prev, s_next, p_high, p_low, n_high, n_low = call(
        functools.partial(kernel_halo, sizes),
        [prev, follow, y0_high, y0_low, y1_high, y1_low, y2_high, y2_low],
        [square, square, half, half, half, half],
        [pltpu.VMEM((2, owners * width, rows * side, side), F32), table, table, pair],
        one * 2,
    )
    return call(
        functools.partial(kernel_last, sizes),
        [inv_3, div, b_high, b_low, p_high, p_low, n_high, n_low, s_own, s_prev, s_next],
        [result],
        [m_half, m_half, table, table, pair],
        one * 2,
    )


def solution(mesh):
    blocks = P(("row", "col"), None, None, None)
    table = P(("row", "col"), None)
    line = P(("row", "col"))
    return jax.shard_map(
        local,
        mesh=mesh,
        in_specs=(blocks, table, table, line, blocks, table, line, table, line),
        out_specs=blocks,
        check_vma=False,
    )
```

```python
import functools

import jax
import jax.numpy as jnp
from jax import lax
from jax.experimental import pallas as pl
from jax.experimental.pallas import tpu as pltpu
from jax.sharding import PartitionSpec as P

F32 = jnp.float32
BF16 = jnp.bfloat16
VMEM = pl.BlockSpec(memory_space=pltpu.VMEM)
SMEM = pl.BlockSpec(memory_space=pltpu.SMEM)
PACK_LIMIT = 60 << 20
PARTS = 4


def halves(value):
    high = value.astype(BF16)
    return high, (value - high.astype(F32)).astype(BF16)


def product(left, right, transposed=False):
    dims = (((1,), (1 if transposed else 0,)), ((), ()))
    dot = functools.partial(lax.dot_general, dimension_numbers=dims, preferred_element_type=F32)
    return dot(left[0], right[0]) + (dot(left[0], right[1]) + dot(left[1], right[0]))


def clear(ref):
    ref[...] = jnp.zeros(ref.shape, ref.dtype)


def place_div(codes, blocks, sizes, dense):
    rows, slots, _, _, side = sizes
    for row in range(rows):
        for slot in range(slots):
            code = codes[row * slots + slot]

            @pl.when(code >= 0)
            def _():
                dense[code, pl.ds(row * side, side), :] += blocks[pl.ds((row * slots + slot) * side, side), :]


def place_inv(codes, blocks, sizes, high, low):
    _, _, width, slots, side = sizes
    for row in range(width):
        for slot in range(slots):
            code = codes[row * slots + slot]

            @pl.when(code >= 0)
            def _():
                spot = (pl.ds(row * side, side), pl.ds(pl.multiple_of(code * side, side), side))
                high[spot], low[spot] = halves(blocks[pl.ds((row * slots + slot) * side, side), :])


def owner_part(dense, owner, width):
    return halves(jnp.concatenate([dense[owner * width + i] for i in range(width)], axis=1))


def write(out, buf, sums, slots, codes, sems):
    rows, pattern, side, _ = out.shape
    copies = []
    for row in range(rows):
        for slot in slots:
            code = codes[row * pattern + slot]
            result = jnp.zeros((side, side), F32)
            for other in range(rows):
                block = sums[row * side : (row + 1) * side, other * side : (other + 1) * side]
                result = jnp.where(code == other, block, result)
            buf[row, slot] = result
            copies.append(pltpu.make_async_copy(buf.at[row, slot], out.at[row, slot], sems.at[row, slot]))
            copies[-1].start()
    return copies


def fetch(sources, targets, sems):
    copies = [pltpu.make_async_copy(x, y, sems.at[i]) for i, (x, y) in enumerate(zip(sources, targets))]
    for copy in copies:
        copy.start()
    return copies


def kernel_pack(inv, div, *refs):
    tables, (inv_out, div_out, tile_out), scratch = refs[:7], refs[7:10], refs[10:]
    small_refs, (inv_buf, div_buf, small_sem, in_sem, out_sem) = scratch[:7], scratch[7:]
    small = fetch(tables, small_refs, small_sem)
    parts = in_sem.shape[1]
    arrays = ((inv, inv_buf, inv_out), (div, div_buf, div_out))
    cuts = [[pl.ds(j * (x.shape[0] // parts), x.shape[0] // parts) for j in range(parts)] for x in (inv, div)]
    reads, writes = [], []
    for i, (blocks, buf, out) in enumerate(arrays):
        reads += fetch([blocks.at[cut] for cut in cuts[i]], [buf.at[cut] for cut in cuts[i]], in_sem.at[i])
    for copy in small:
        copy.wait()
    for i, tables in enumerate((small_refs[:2], small_refs[2:])):
        _, buf, out = arrays[i]
        at = rows = buf.shape[0] - 8
        buf[pl.ds(rows, 8), :] = jnp.zeros((8, buf.shape[1]), F32)
        for table in tables:
            values = table[...].astype(F32)
            height, length = (1, *values.shape)[-2:]
            buf[pl.ds(at, height), pl.ds(0, length)] = values.reshape(height, length)
            at += height
        cuts[i].append(pl.ds(rows, 8))
    tile = pltpu.make_async_copy(inv_buf.at[cuts[0][-1]], tile_out, small_sem.at[0])
    tile.start()
    writes.append(tile)
    for i, (_, buf, out) in enumerate(arrays):
        for j, cut in enumerate(cuts[i]):
            if j < parts:
                reads[i * parts + j].wait()
            copy = pltpu.make_async_copy(buf.at[cut], out.at[cut], out_sem.at[i, j])
            copy.start()
            writes.append(copy)
    for copy in writes:
        copy.wait()


def integers(packed):
    return packed[pl.ds(packed.shape[0] - 8, 8), :].astype(jnp.int32)


def inv_codes(table, sizes):
    _, _, width, slots, _ = sizes
    codes = []
    for u in range(width):
        count = table[width, u]
        codes += [jnp.where(m < count, table[u, m], -1) for m in range(slots)]
    return codes


def div_codes(table, sizes):
    rows, slots, width, _, _ = sizes
    mine = lax.axis_index("row")
    odd = lax.axis_index("col") % 2
    codes = []
    for i in range(rows):
        count = table[3 * rows, i]
        for k in range(slots):
            apart = table[i, k] ^ mine
            apart = jnp.where(odd == 1, ((apart & 1) << 1) | (apart >> 1), apart)
            code = apart * width + table[rows + i, k]
            codes.append(jnp.where(k < count, code, -1))
    return codes


def target_codes(table, rows, pattern):
    codes = []
    for i in range(rows):
        count = table[3 * rows + 1, i]
        codes += [jnp.where(t < count, table[2 * rows + i, t] % rows, -1) for t in range(pattern)]
    return codes


def read_inv(inv, tile, sizes, m_high, m_low):
    clear(m_high)
    clear(m_low)
    place_inv(inv_codes(integers(tile), sizes), inv, sizes, m_high, m_low)


def kernel_own(sizes, div, inv, b_high, b_low, y_high, y_low, s_own, dense, m_high, m_low):
    clear(dense)
    read_inv(inv, inv, sizes, m_high, m_low)
    place_div(div_codes(integers(div), sizes), div, sizes, dense)
    for owner in range(b_high.shape[0]):
        b_high[owner], b_low[owner] = owner_part(dense, owner, sizes[2])
    own = (b_high[0], b_low[0])
    y_high[...], y_low[...] = halves(product(own, (m_high[...], m_low[...])))
    size = own[0].shape[1]
    s_own[...] = product((y_high[:, size : 2 * size], y_low[:, size : 2 * size]), own, True)


def kernel_side(which, sizes, inv, tile, b_high, b_low, s_in, y_high, y_low, s_out, m_high, m_low):
    read_inv(inv, tile, sizes, m_high, m_low)
    part = (b_high[which], b_low[which])
    y_high[...], y_low[...] = halves(product(part, (m_high[...], m_low[...])))
    size = part[0].shape[1]
    s_out[...] = s_in[...] + product((y_high[:, size : 2 * size], y_low[:, size : 2 * size]), part, True)


def kernel_next(sizes, y0_high, y0_low, y1_high, y1_low, y2_high, y2_low, div, s_next, n_high, n_low, dense):
    clear(dense)
    place_div(div_codes(integers(div), sizes), div, sizes, dense)
    size = n_high.shape[1]
    cut = slice(2 * size, 3 * size)
    for owner, (high, low) in enumerate(((y0_high, y0_low), (y1_high, y1_low), (y2_high, y2_low))):
        term = product((high[:, cut], low[:, cut]), owner_part(dense, owner, sizes[2]), True)
        s_next[...] = term if owner == 0 else s_next[...] + term
    n_high[...], n_low[...] = owner_part(dense, 3, sizes[2])


def kernel_far(
    sizes, inv, tile, div, b_high, b_low, n_high, n_low, s_own, s_next, out, y3_high, y3_low, m_high, m_low, buf, out_sem
):
    read_inv(inv, tile, sizes, m_high, m_low)
    codes = target_codes(integers(div), *out.shape[:2])
    own = (b_high[3], b_low[3])
    y_high, y_low = halves(product(own, (m_high[...], m_low[...])))
    size = own[0].shape[1]
    y3_high[...], y3_low[...] = y_high[:, :size], y_low[:, :size]
    cut = slice(size, 2 * size)
    own_sum = s_own[...] + product((y_high[:, cut], y_low[:, cut]), own, True)
    copies = write(out, buf, own_sum, (0, 1), codes, out_sem)
    cut = slice(2 * size, 3 * size)
    next_sum = s_next[...] + product((y_high[:, cut], y_low[:, cut]), (n_high[...], n_low[...]), True)
    copies += write(out, buf, next_sum, (2,), codes, out_sem)
    for copy in copies:
        copy.wait()


def kernel_prev(sizes, ready, div, own, *refs):
    ys, (out, buf, dense, out_sem) = refs[:8], refs[8:]
    clear(dense)
    place_div(div_codes(integers(div), sizes), div, sizes, dense)
    size = dense.shape[1]
    total = None
    for owner in range(4):
        term = product((ys[2 * owner][:, :size], ys[2 * owner + 1][:, :size]), owner_part(dense, owner, sizes[2]), True)
        total = term if owner == 0 else total + term
    for copy in write(out, buf, total, (3,), target_codes(integers(own), *out.shape[:2]), out_sem):
        copy.wait()


def kernel_all(sizes, d_meta, p_meta, n_meta, m_meta, s_meta, div, prev, follow, inv, out, dense, sums, m_high, m_low, buf, out_sem):
    _, _, width, slots, _ = sizes
    clear(dense)
    clear(sums)
    for region, (meta, blocks) in enumerate(((p_meta, prev), (d_meta, div), (n_meta, follow))):
        place_div(meta, blocks, sizes, dense.at[region])

    @pl.loop(0, inv.shape[0])
    def _(owner):
        clear(m_high)
        clear(m_low)
        codes = [m_meta[owner * width * slots + i] for i in range(width * slots)]
        place_inv(codes, inv.at[owner], sizes, m_high, m_low)
        size = m_high.shape[0]
        own = owner_part(dense.at[1], owner, width)
        y_high, y_low = halves(product(own, (m_high[...], m_low[...])))
        for region in range(3):
            cut = slice(region * size, (region + 1) * size)
            sums[region] += product((y_high[:, cut], y_low[:, cut]), owner_part(dense.at[region], owner, width), True)

    codes = [s_meta[i] for i in range(out.shape[0] * out.shape[1])]
    for slots, region in (((0, 1), 1), ((2,), 2), ((3,), 0)):
        for copy in write(out, buf, sums[region], slots, codes, out_sem):
            copy.wait()


def call(kernel, operands, outs, scratch, flops, scalars=0, specs=None, out_specs=None, aliases=None, limit=24 << 20):
    moved = sum(x.size * x.dtype.itemsize for x in operands[scalars:] + outs)
    return pl.pallas_call(
        kernel,
        out_shape=outs if len(outs) > 1 else outs[0],
        in_specs=specs or [SMEM] * scalars + [VMEM] * (len(operands) - scalars),
        out_specs=out_specs or ([VMEM] * len(outs) if len(outs) > 1 else VMEM),
        scratch_shapes=scratch,
        input_output_aliases=aliases or {},
        compiler_params=pltpu.CompilerParams(vmem_limit_bytes=limit),
        cost_estimate=pl.CostEstimate(flops=flops, bytes_accessed=moved, transcendentals=0),
    )(*operands)


def local(div_blocks, div_owner, div_local, div_count, inv_blocks, inv_cols, inv_count, schur_cols, schur_count):
    rows, slots, side, _ = div_blocks.shape
    width, inv_slots = inv_cols.shape
    pattern = schur_cols.shape[1]
    owners = lax.axis_size("row")
    count = lax.axis_size("col")
    size, wide = width * side, 3 * width * side
    sizes = (rows, slots, width, inv_slots, side)
    forward = [(i, (i + 1) % count) for i in range(count)]
    backward = [(i, (i - 1) % count) for i in range(count)]
    div_flat = div_blocks.reshape(rows * slots * side, side)
    inv_flat = inv_blocks.reshape(width * inv_slots * side, side)

    square = jax.ShapeDtypeStruct((rows * side, rows * side), F32)
    half = jax.ShapeDtypeStruct((rows * side, size), BF16)
    every = jax.ShapeDtypeStruct((owners, rows * side, size), BF16)
    y_half = jax.ShapeDtypeStruct((rows * side, wide), BF16)
    result = jax.ShapeDtypeStruct((rows, pattern, side, side), F32)
    m_half = pltpu.VMEM((size, wide), BF16)
    one = 2 * 3 * rows * side * size * wide

    if owners != 4 or count % 2 or rows != 2 or side != 128:

        def order(length):
            return jnp.arange(length, dtype=jnp.int32)[None, :]

        d_meta = jnp.where(order(slots) < div_count[:, None], div_owner * width + div_local, -1).reshape(-1)
        m_meta = jnp.where(order(inv_slots) < inv_count[:, None], inv_cols, -1).reshape(-1)
        s_meta = jnp.where(order(pattern) < schur_count[:, None], schur_cols % rows, -1).reshape(-1)
        prev = lax.ppermute(div_flat, "col", forward)
        follow = lax.ppermute(div_flat, "col", backward)
        p_meta = lax.ppermute(d_meta, "col", forward)
        n_meta = lax.ppermute(d_meta, "col", backward)
        inv = lax.all_gather(inv_flat, "row")
        all_meta = lax.all_gather(m_meta, "row", tiled=True)
        return call(
            functools.partial(kernel_all, sizes),
            [d_meta, p_meta, n_meta, all_meta, s_meta, div_flat, prev, follow, inv],
            [result],
            [
                pltpu.VMEM((3, owners * width, rows * side, side), F32),
                pltpu.VMEM((3, rows * side, rows * side), F32),
                m_half,
                m_half,
                pltpu.VMEM(result.shape, F32),
                pltpu.SemaphoreType.DMA((rows, pattern)),
            ],
            owners * one * 2,
            scalars=5,
            out_specs=pl.BlockSpec(memory_space=pl.ANY),
            limit=56 << 20,
        )

    anywhere = pl.BlockSpec(memory_space=pl.ANY)

    tables = (inv_cols, inv_count, div_owner, div_local, schur_cols, div_count, schur_count)
    packed = [jax.ShapeDtypeStruct((x.shape[0] + 8, side), F32) for x in (inv_flat, div_flat)]
    inv, div, tile = call(
        kernel_pack,
        [inv_flat, div_flat, *tables],
        [*packed, jax.ShapeDtypeStruct((8, side), F32)],
        [pltpu.VMEM(x.shape, x.dtype) for x in (*tables, *packed)]
        + [pltpu.SemaphoreType.DMA(shape) for shape in ((len(tables),), (2, PARTS), (2, PARTS + 1))],
        0,
        specs=[anywhere] * (2 + len(tables)),
        out_specs=[anywhere] * 3,
        limit=PACK_LIMIT,
    )

    def swap(first):
        def partner(r, c):
            return r ^ (1 if (c % 2 == 0) == first else 2)

        return [(r * count + c, partner(r, c) * count + c) for r in range(owners) for c in range(count)]

    inv_1 = lax.ppermute(inv_flat, ("row", "col"), swap(True))
    inv_2 = lax.ppermute(inv, ("row", "col"), swap(False))
    follow = lax.ppermute(div, "col", backward)
    prev = lax.ppermute(div, "col", forward)

    m_scratch = [m_half, m_half]
    b_high, b_low, y0_high, y0_low, s_own = call(
        functools.partial(kernel_own, sizes),
        [div, inv],
        [every, every, y_half, y_half, square],
        [pltpu.VMEM((owners * width, rows * side, side), F32), *m_scratch],
        one * 4 // 3,
    )
    inv_1, s_own = lax.optimization_barrier((inv_1, s_own))
    inv_3 = lax.ppermute(inv_1, ("row", "col"), swap(False))
    tile_1 = lax.ppermute(tile, ("row", "col"), swap(True))
    tile_3 = lax.ppermute(tile_1, ("row", "col"), swap(False))
    y1_high, y1_low, s_own = call(
        functools.partial(kernel_side, 1, sizes), [inv_1, tile_1, b_high, b_low, s_own], [y_half, y_half, square], m_scratch, one * 4 // 3
    )
    y2_high, y2_low, s_own = call(
        functools.partial(kernel_side, 2, sizes), [inv_2, inv_2, b_high, b_low, s_own], [y_half, y_half, square], m_scratch, one * 4 // 3
    )
    s_next, n_high, n_low = call(
        functools.partial(kernel_next, sizes),
        [y0_high, y0_low, y1_high, y1_low, y2_high, y2_low, follow],
        [square, half, half],
        [pltpu.VMEM((owners * width, rows * side, side), F32)],
        one,
    )
    out_scratch = [pltpu.VMEM(result.shape, F32)]
    out_sems = pltpu.SemaphoreType.DMA((rows, pattern))
    ready, y3_high, y3_low = call(
        functools.partial(kernel_far, sizes),
        [inv_3, tile_3, div, b_high, b_low, n_high, n_low, s_own, s_next],
        [result, half, half],
        [*m_scratch, *out_scratch, out_sems],
        one * 5 // 3,
        out_specs=[anywhere, VMEM, VMEM],
    )
    return call(
        functools.partial(kernel_prev, sizes),
        [ready, prev, div, y0_high, y0_low, y1_high, y1_low, y2_high, y2_low, y3_high, y3_low],
        [result],
        [*out_scratch, pltpu.VMEM((owners * width, rows * side, side), F32), out_sems],
        one,
        specs=[anywhere] + [VMEM] * 10,
        out_specs=anywhere,
        aliases={0: 0},
    )


def solution(mesh):
    blocks = P(("row", "col"), None, None, None)
    table = P(("row", "col"), None)
    line = P(("row", "col"))
    return jax.shard_map(
        local,
        mesh=mesh,
        in_specs=(blocks, table, table, line, blocks, table, line, table, line),
        out_specs=blocks,
        check_vma=False,
    )
```

```python
import functools

import jax
import jax.numpy as jnp
from jax import lax
from jax.experimental import pallas as pl
from jax.experimental.pallas import tpu as pltpu
from jax.sharding import PartitionSpec as P

F32 = jnp.float32
BF16 = jnp.bfloat16
VMEM = pl.BlockSpec(memory_space=pltpu.VMEM)
SMEM = pl.BlockSpec(memory_space=pltpu.SMEM)
PACK_LIMIT = 60 << 20
PARTS = 4


def halves(value):
    high = value.astype(BF16)
    return high, (value - high.astype(F32)).astype(BF16)


def product(left, right, transposed=False):
    dims = (((1,), (1 if transposed else 0,)), ((), ()))
    dot = functools.partial(lax.dot_general, dimension_numbers=dims, preferred_element_type=F32)
    return dot(left[0], right[0]) + (dot(left[0], right[1]) + dot(left[1], right[0]))


def clear(ref):
    ref[...] = jnp.zeros(ref.shape, ref.dtype)


def place_div(codes, blocks, sizes, dense):
    rows, slots, _, _, side = sizes
    for row in range(rows):
        for slot in range(slots):
            code = codes[row * slots + slot]

            @pl.when(code >= 0)
            def _():
                dense[code, pl.ds(row * side, side), :] += blocks[pl.ds((row * slots + slot) * side, side), :]


def place_inv(codes, blocks, sizes, high, low):
    _, _, width, slots, side = sizes
    for row in range(width):
        for slot in range(slots):
            code = codes[row * slots + slot]

            @pl.when(code >= 0)
            def _():
                spot = (pl.ds(row * side, side), pl.ds(pl.multiple_of(code * side, side), side))
                high[spot], low[spot] = halves(blocks[pl.ds((row * slots + slot) * side, side), :])


def owner_part(dense, owner, width):
    return halves(jnp.concatenate([dense[owner * width + i] for i in range(width)], axis=1))


def pick(out, sums, slots, codes):
    rows, _, side, _ = out.shape
    pattern = len(codes) // rows
    for row in range(rows):
        for slot in slots:
            code = codes[row * pattern + slot]
            result = jnp.zeros((side, side), F32)
            for other in range(rows):
                block = sums[row * side : (row + 1) * side, other * side : (other + 1) * side]
                result = jnp.where(code == other, block, result)
            out[row, slot] = result


def fetch(sources, targets, sems):
    copies = [pltpu.make_async_copy(x, y, sems.at[i]) for i, (x, y) in enumerate(zip(sources, targets))]
    for copy in copies:
        copy.start()
    return copies


def kernel_pack(inv, div, *refs):
    tables, (inv_out, div_out, tile_out), scratch = refs[:7], refs[7:10], refs[10:]
    small_refs, (inv_buf, div_buf, small_sem, in_sem, out_sem) = scratch[:7], scratch[7:]
    small = fetch(tables, small_refs, small_sem)
    parts = in_sem.shape[1]
    arrays = ((inv, inv_buf, inv_out), (div, div_buf, div_out))
    cuts = [[pl.ds(j * (x.shape[0] // parts), x.shape[0] // parts) for j in range(parts)] for x in (inv, div)]
    reads, writes = [], []
    for i, (blocks, buf, out) in enumerate(arrays):
        reads += fetch([blocks.at[cut] for cut in cuts[i]], [buf.at[cut] for cut in cuts[i]], in_sem.at[i])
    for copy in small:
        copy.wait()
    for i, tables in enumerate((small_refs[:2], small_refs[2:])):
        _, buf, out = arrays[i]
        at = rows = buf.shape[0] - 8
        buf[pl.ds(rows, 8), :] = jnp.zeros((8, buf.shape[1]), F32)
        for table in tables:
            values = table[...].astype(F32)
            height, length = (1, *values.shape)[-2:]
            buf[pl.ds(at, height), pl.ds(0, length)] = values.reshape(height, length)
            at += height
        cuts[i].append(pl.ds(rows, 8))
    tile = pltpu.make_async_copy(inv_buf.at[cuts[0][-1]], tile_out, small_sem.at[0])
    tile.start()
    writes.append(tile)
    for i, (_, buf, out) in enumerate(arrays):
        for j, cut in enumerate(cuts[i]):
            if j < parts:
                reads[i * parts + j].wait()
            copy = pltpu.make_async_copy(buf.at[cut], out.at[cut], out_sem.at[i, j])
            copy.start()
            writes.append(copy)
    for copy in writes:
        copy.wait()


def integers(packed):
    return packed[pl.ds(packed.shape[0] - 8, 8), :].astype(jnp.int32)


def inv_codes(table, sizes):
    _, _, width, slots, _ = sizes
    codes = []
    for u in range(width):
        count = table[width, u]
        codes += [jnp.where(m < count, table[u, m], -1) for m in range(slots)]
    return codes


def div_codes(table, sizes):
    rows, slots, width, _, _ = sizes
    mine = lax.axis_index("row")
    odd = lax.axis_index("col") % 2
    codes = []
    for i in range(rows):
        count = table[2 * rows, i]
        for k in range(slots):
            apart = table[i, k] ^ mine
            apart = jnp.where(odd == 1, ((apart & 1) << 1) | (apart >> 1), apart)
            code = apart * width + table[rows + i, k]
            codes.append(jnp.where(k < count, code, -1))
    return codes


def target_codes(table, rows, pattern):
    codes = []
    for i in range(rows):
        count = table[rows, i]
        codes += [jnp.where(t < count, table[i, t] % rows, -1) for t in range(pattern)]
    return codes


def read_inv(inv, tile, sizes, m_high, m_low):
    clear(m_high)
    clear(m_low)
    place_inv(inv_codes(integers(tile), sizes), inv, sizes, m_high, m_low)


def kernel_own(sizes, div, inv, b_high, b_low, y_high, y_low, s_own, dense, m_high, m_low):
    clear(dense)
    read_inv(inv, inv, sizes, m_high, m_low)
    place_div(div_codes(integers(div), sizes), div, sizes, dense)
    for owner in range(b_high.shape[0]):
        b_high[owner], b_low[owner] = owner_part(dense, owner, sizes[2])
    own = (b_high[0], b_low[0])
    y_high[...], y_low[...] = halves(product(own, (m_high[...], m_low[...])))
    size = own[0].shape[1]
    s_own[...] = product((y_high[:, size : 2 * size], y_low[:, size : 2 * size]), own, True)


def kernel_side(which, sizes, inv, tile, b_high, b_low, s_in, y_high, y_low, s_out, m_high, m_low):
    read_inv(inv, tile, sizes, m_high, m_low)
    part = (b_high[which], b_low[which])
    y_high[...], y_low[...] = halves(product(part, (m_high[...], m_low[...])))
    size = part[0].shape[1]
    s_out[...] = s_in[...] + product((y_high[:, size : 2 * size], y_low[:, size : 2 * size]), part, True)


def kernel_next(sizes, y0_high, y0_low, y1_high, y1_low, y2_high, y2_low, div, s_next, n_high, n_low, p_high, p_low, dense):
    width, side = sizes[2], sizes[4]
    clear(dense)
    place_div(div_codes(integers(div), sizes), div, sizes, dense)
    size = n_high.shape[1]
    cut = slice(2 * size, 3 * size)
    for owner, (high, low) in enumerate(((y0_high, y0_low), (y1_high, y1_low), (y2_high, y2_low))):
        term = product((high[:, cut], low[:, cut]), owner_part(dense, owner, width), True)
        s_next[...] = term if owner == 0 else s_next[...] + term
        for u in range(width):
            block = slice(u * side, (u + 1) * side)
            p_high[owner * width + u], p_low[owner * width + u] = high[:, block], low[:, block]
    n_high[...], n_low[...] = owner_part(dense, 3, width)


def kernel_far(
    sizes, inv, tile, div, b_high, b_low, n_high, n_low, s_own, s_next, p_in_high, p_in_low, blocks, p_high, p_low, m_high, m_low
):
    rows, _, width, _, side = sizes
    read_inv(inv, tile, sizes, m_high, m_low)
    codes = target_codes(integers(div), rows, blocks.shape[1] + 1)
    own = (b_high[3], b_low[3])
    y_high, y_low = halves(product(own, (m_high[...], m_low[...])))
    size = own[0].shape[1]
    for u in range(width):
        cut = slice(u * side, (u + 1) * side)
        p_high[3 * width + u], p_low[3 * width + u] = y_high[:, cut], y_low[:, cut]
    cut = slice(size, 2 * size)
    own_sum = s_own[...] + product((y_high[:, cut], y_low[:, cut]), own, True)
    pick(blocks, own_sum, (0, 1), codes)
    cut = slice(2 * size, 3 * size)
    next_sum = s_next[...] + product((y_high[:, cut], y_low[:, cut]), (n_high[...], n_low[...]), True)
    pick(blocks, next_sum, (2,), codes)


def kernel_prev(sizes, div, own, p_high, p_low, blocks, out, buf, left_high, left_low, sems):
    rows, slots, _, _, side = sizes
    pattern = out.shape[1]
    copies = []
    for row in range(rows):
        copies.append(pltpu.make_async_copy(blocks.at[row], out.at[row, pl.ds(0, pattern - 1)], sems.at[0, row]))
        copies[-1].start()
    codes = div_codes(integers(div), sizes)
    targets = target_codes(integers(own), rows, pattern)
    for row in range(rows):
        target = targets[row * pattern + pattern - 1]
        place = pl.ds(row * side, side)
        other = jnp.maximum(target, 0)
        right = []
        for slot in range(slots):
            code = codes[slot]
            for i in range(1, rows):
                code = jnp.where(other == i, codes[i * slots + slot], code)
            cut = pl.ds(slot * side, side)
            source = pl.multiple_of((other * slots + slot) * side, side)
            live = jnp.where((code >= 0) & (target >= 0), 1.0, 0.0)
            right.append(div[pl.ds(source, side), :] * live)
            code = jnp.maximum(code, 0)
            left_high[:, cut], left_low[:, cut] = p_high[code, place, :], p_low[code, place, :]
        buf[row] = product((left_high[...], left_low[...]), halves(jnp.concatenate(right, axis=1)), True)
        copies.append(pltpu.make_async_copy(buf.at[row], out.at[row, pattern - 1], sems.at[1, row]))
        copies[-1].start()
    for copy in copies:
        copy.wait()


def kernel_all(sizes, d_meta, p_meta, n_meta, m_meta, s_meta, div, prev, follow, inv, out, dense, sums, m_high, m_low):
    _, _, width, slots, _ = sizes
    clear(dense)
    clear(sums)
    for region, (meta, blocks) in enumerate(((p_meta, prev), (d_meta, div), (n_meta, follow))):
        place_div(meta, blocks, sizes, dense.at[region])

    @pl.loop(0, inv.shape[0])
    def _(owner):
        clear(m_high)
        clear(m_low)
        codes = [m_meta[owner * width * slots + i] for i in range(width * slots)]
        place_inv(codes, inv.at[owner], sizes, m_high, m_low)
        size = m_high.shape[0]
        own = owner_part(dense.at[1], owner, width)
        y_high, y_low = halves(product(own, (m_high[...], m_low[...])))
        for region in range(3):
            cut = slice(region * size, (region + 1) * size)
            sums[region] += product((y_high[:, cut], y_low[:, cut]), owner_part(dense.at[region], owner, width), True)

    codes = [s_meta[i] for i in range(out.shape[0] * out.shape[1])]
    for slots, region in (((0, 1), 1), ((2,), 2), ((3,), 0)):
        pick(out, sums[region], slots, codes)


def call(kernel, operands, outs, scratch, flops, scalars=0, specs=None, out_specs=None, aliases=None, limit=24 << 20):
    moved = sum(x.size * x.dtype.itemsize for x in operands[scalars:] + outs)
    return pl.pallas_call(
        kernel,
        out_shape=outs if len(outs) > 1 else outs[0],
        in_specs=specs or [SMEM] * scalars + [VMEM] * (len(operands) - scalars),
        out_specs=out_specs or ([VMEM] * len(outs) if len(outs) > 1 else VMEM),
        scratch_shapes=scratch,
        input_output_aliases=aliases or {},
        compiler_params=pltpu.CompilerParams(vmem_limit_bytes=limit),
        cost_estimate=pl.CostEstimate(flops=flops, bytes_accessed=moved, transcendentals=0),
    )(*operands)


def local(div_blocks, div_owner, div_local, div_count, inv_blocks, inv_cols, inv_count, schur_cols, schur_count):
    rows, slots, side, _ = div_blocks.shape
    width, inv_slots = inv_cols.shape
    pattern = schur_cols.shape[1]
    owners = lax.axis_size("row")
    count = lax.axis_size("col")
    size, wide = width * side, 3 * width * side
    sizes = (rows, slots, width, inv_slots, side)
    forward = [(i, (i + 1) % count) for i in range(count)]
    backward = [(i, (i - 1) % count) for i in range(count)]
    div_flat = div_blocks.reshape(rows * slots * side, side)
    inv_flat = inv_blocks.reshape(width * inv_slots * side, side)

    square = jax.ShapeDtypeStruct((rows * side, rows * side), F32)
    half = jax.ShapeDtypeStruct((rows * side, size), BF16)
    every = jax.ShapeDtypeStruct((owners, rows * side, size), BF16)
    y_half = jax.ShapeDtypeStruct((rows * side, wide), BF16)
    result = jax.ShapeDtypeStruct((rows, pattern, side, side), F32)
    m_half = pltpu.VMEM((size, wide), BF16)
    one = 2 * 3 * rows * side * size * wide

    if owners != 4 or count % 2 or rows != 2 or side != 128 or pattern != 4:

        def order(length):
            return jnp.arange(length, dtype=jnp.int32)[None, :]

        d_meta = jnp.where(order(slots) < div_count[:, None], div_owner * width + div_local, -1).reshape(-1)
        m_meta = jnp.where(order(inv_slots) < inv_count[:, None], inv_cols, -1).reshape(-1)
        s_meta = jnp.where(order(pattern) < schur_count[:, None], schur_cols % rows, -1).reshape(-1)
        prev = lax.ppermute(div_flat, "col", forward)
        follow = lax.ppermute(div_flat, "col", backward)
        p_meta = lax.ppermute(d_meta, "col", forward)
        n_meta = lax.ppermute(d_meta, "col", backward)
        inv = lax.all_gather(inv_flat, "row")
        all_meta = lax.all_gather(m_meta, "row", tiled=True)
        return call(
            functools.partial(kernel_all, sizes),
            [d_meta, p_meta, n_meta, all_meta, s_meta, div_flat, prev, follow, inv],
            [result],
            [
                pltpu.VMEM((3, owners * width, rows * side, side), F32),
                pltpu.VMEM((3, rows * side, rows * side), F32),
                m_half,
                m_half,
            ],
            owners * one * 2,
            scalars=5,
            limit=56 << 20,
        )

    anywhere = pl.BlockSpec(memory_space=pl.ANY)

    def noted(blocks, tables):
        height = blocks.shape[0] + 8
        out, at = jnp.pad(blocks, ((0, 8), (0, 0))), blocks.shape[0]
        for table in tables:
            lines, length = table.shape
            out = out + jnp.pad(table.astype(F32), ((at, height - at - lines), (0, side - length)))
            at += lines
        return out

    inv_tables = (inv_cols, inv_count[None, :])
    div = noted(div_flat, (div_owner, div_local, div_count[None, :]))
    inv = noted(inv_flat, inv_tables)
    nothing = jnp.zeros((0, side), F32)
    tile = noted(nothing, inv_tables)
    pattern_tile = noted(nothing, (schur_cols, schur_count[None, :]))

    def swap(first):
        def partner(r, c):
            return r ^ (1 if (c % 2 == 0) == first else 2)

        return [(r * count + c, partner(r, c) * count + c) for r in range(owners) for c in range(count)]

    inv_1 = lax.ppermute(inv_flat, ("row", "col"), swap(True))
    inv_2 = lax.ppermute(inv, ("row", "col"), swap(False))
    follow = lax.ppermute(div, "col", backward)
    prev = lax.ppermute(div, "col", forward)

    m_scratch = [m_half, m_half]
    b_high, b_low, y0_high, y0_low, s_own = call(
        functools.partial(kernel_own, sizes),
        [div, inv],
        [every, every, y_half, y_half, square],
        [pltpu.VMEM((owners * width, rows * side, side), F32), *m_scratch],
        one * 4 // 3,
    )
    inv_1, s_own = lax.optimization_barrier((inv_1, s_own))
    inv_3 = lax.ppermute(inv_1, ("row", "col"), swap(False))
    tile_1 = lax.ppermute(tile, ("row", "col"), swap(True))
    tile_3 = lax.ppermute(tile_1, ("row", "col"), swap(False))
    y1_high, y1_low, s_own = call(
        functools.partial(kernel_side, 1, sizes), [inv_1, tile_1, b_high, b_low, s_own], [y_half, y_half, square], m_scratch, one * 4 // 3
    )
    y2_high, y2_low, s_own = call(
        functools.partial(kernel_side, 2, sizes), [inv_2, inv_2, b_high, b_low, s_own], [y_half, y_half, square], m_scratch, one * 4 // 3
    )
    p_half = jax.ShapeDtypeStruct((owners * width, rows * side, side), BF16)
    s_next, n_high, n_low, p_high, p_low = call(
        functools.partial(kernel_next, sizes),
        [y0_high, y0_low, y1_high, y1_low, y2_high, y2_low, follow],
        [square, half, half, p_half, p_half],
        [pltpu.VMEM((owners * width, rows * side, side), F32)],
        one,
    )
    three, p_high, p_low = call(
        functools.partial(kernel_far, sizes),
        [inv_3, tile_3, pattern_tile, b_high, b_low, n_high, n_low, s_own, s_next, p_high, p_low],
        [jax.ShapeDtypeStruct((rows, pattern - 1, side, side), F32), p_half, p_half],
        m_scratch,
        one * 5 // 3,
        aliases={9: 1, 10: 2},
    )
    left = pltpu.VMEM((side, slots * side), BF16)
    return call(
        functools.partial(kernel_prev, sizes),
        [prev, pattern_tile, p_high, p_low, three],
        [result],
        [pltpu.VMEM((rows, side, side), F32), left, left, pltpu.SemaphoreType.DMA((2, rows))],
        one,
        out_specs=anywhere,
    )


def solution(mesh):
    blocks = P(("row", "col"), None, None, None)
    table = P(("row", "col"), None)
    line = P(("row", "col"))
    return jax.shard_map(
        local,
        mesh=mesh,
        in_specs=(blocks, table, table, line, blocks, table, line, table, line),
        out_specs=blocks,
        check_vma=False,
    )
```

```python
import functools

import jax
import jax.numpy as jnp
from jax import lax
from jax.experimental import pallas as pl
from jax.experimental.pallas import tpu as pltpu
from jax.sharding import PartitionSpec as P

F32 = jnp.float32
BF16 = jnp.bfloat16
VMEM = pl.BlockSpec(memory_space=pltpu.VMEM)
SMEM = pl.BlockSpec(memory_space=pltpu.SMEM)
PACK_LIMIT = 60 << 20
PARTS = 4


def halves(value):
    high = value.astype(BF16)
    return high, (value - high.astype(F32)).astype(BF16)


def product(left, right, transposed=False):
    dims = (((1,), (1 if transposed else 0,)), ((), ()))
    dot = functools.partial(lax.dot_general, dimension_numbers=dims, preferred_element_type=F32)
    return dot(left[0], right[0]) + (dot(left[0], right[1]) + dot(left[1], right[0]))


def clear(ref):
    ref[...] = jnp.zeros(ref.shape, ref.dtype)


def place_div(codes, blocks, sizes, dense):
    rows, slots, _, _, side = sizes
    for row in range(rows):
        for slot in range(slots):
            code = codes[row * slots + slot]

            @pl.when(code >= 0)
            def _():
                dense[code, pl.ds(row * side, side), :] += blocks[pl.ds((row * slots + slot) * side, side), :]


def place_inv(codes, blocks, sizes, high, low):
    _, _, width, slots, side = sizes
    for row in range(width):
        for slot in range(slots):
            code = codes[row * slots + slot]

            @pl.when(code >= 0)
            def _():
                spot = (pl.ds(row * side, side), pl.ds(pl.multiple_of(code * side, side), side))
                high[spot], low[spot] = halves(blocks[pl.ds((row * slots + slot) * side, side), :])


def owner_part(dense, owner, width):
    return halves(jnp.concatenate([dense[owner * width + i] for i in range(width)], axis=1))


def pick(out, sums, slots, codes):
    rows, _, side, _ = out.shape
    pattern = len(codes) // rows
    for row in range(rows):
        for slot in slots:
            code = codes[row * pattern + slot]
            result = jnp.zeros((side, side), F32)
            for other in range(rows):
                block = sums[row * side : (row + 1) * side, other * side : (other + 1) * side]
                result = jnp.where(code == other, block, result)
            out[row, slot] = result


def fetch(sources, targets, sems):
    copies = [pltpu.make_async_copy(x, y, sems.at[i]) for i, (x, y) in enumerate(zip(sources, targets))]
    for copy in copies:
        copy.start()
    return copies


def kernel_pack(inv, div, *refs):
    tables, (inv_out, div_out, tile_out), scratch = refs[:7], refs[7:10], refs[10:]
    small_refs, (inv_buf, div_buf, small_sem, in_sem, out_sem) = scratch[:7], scratch[7:]
    small = fetch(tables, small_refs, small_sem)
    parts = in_sem.shape[1]
    arrays = ((inv, inv_buf, inv_out), (div, div_buf, div_out))
    cuts = [[pl.ds(j * (x.shape[0] // parts), x.shape[0] // parts) for j in range(parts)] for x in (inv, div)]
    reads, writes = [], []
    for i, (blocks, buf, out) in enumerate(arrays):
        reads += fetch([blocks.at[cut] for cut in cuts[i]], [buf.at[cut] for cut in cuts[i]], in_sem.at[i])
    for copy in small:
        copy.wait()
    for i, tables in enumerate((small_refs[:2], small_refs[2:])):
        _, buf, out = arrays[i]
        at = rows = buf.shape[0] - 8
        buf[pl.ds(rows, 8), :] = jnp.zeros((8, buf.shape[1]), F32)
        for table in tables:
            values = table[...].astype(F32)
            height, length = (1, *values.shape)[-2:]
            buf[pl.ds(at, height), pl.ds(0, length)] = values.reshape(height, length)
            at += height
        cuts[i].append(pl.ds(rows, 8))
    tile = pltpu.make_async_copy(inv_buf.at[cuts[0][-1]], tile_out, small_sem.at[0])
    tile.start()
    writes.append(tile)
    for i, (_, buf, out) in enumerate(arrays):
        for j, cut in enumerate(cuts[i]):
            if j < parts:
                reads[i * parts + j].wait()
            copy = pltpu.make_async_copy(buf.at[cut], out.at[cut], out_sem.at[i, j])
            copy.start()
            writes.append(copy)
    for copy in writes:
        copy.wait()


def integers(packed):
    return packed[pl.ds(packed.shape[0] - 8, 8), :].astype(jnp.int32)


def inv_codes(table, sizes):
    _, _, width, slots, _ = sizes
    codes = []
    for u in range(width):
        count = table[width, u]
        codes += [jnp.where(m < count, table[u, m], -1) for m in range(slots)]
    return codes


def div_codes(table, sizes):
    rows, slots, width, _, _ = sizes
    mine = lax.axis_index("row")
    odd = lax.axis_index("col") % 2
    codes = []
    for i in range(rows):
        count = table[2 * rows, i]
        for k in range(slots):
            apart = table[i, k] ^ mine
            apart = jnp.where(odd == 1, ((apart & 1) << 1) | (apart >> 1), apart)
            code = apart * width + table[rows + i, k]
            codes.append(jnp.where(k < count, code, -1))
    return codes


def target_codes(table, rows, pattern):
    codes = []
    for i in range(rows):
        count = table[rows, i]
        codes += [jnp.where(t < count, table[i, t] % rows, -1) for t in range(pattern)]
    return codes


def read_inv(inv, tile, sizes, m_high, m_low):
    clear(m_high)
    clear(m_low)
    place_inv(inv_codes(integers(tile), sizes), inv, sizes, m_high, m_low)


def kernel_own(sizes, div, inv, b_high, b_low, y_high, y_low, s_own, dense, m_high, m_low):
    clear(dense)
    read_inv(inv, inv, sizes, m_high, m_low)
    place_div(div_codes(integers(div), sizes), div, sizes, dense)
    for owner in range(b_high.shape[0]):
        b_high[owner], b_low[owner] = owner_part(dense, owner, sizes[2])
    own = (b_high[0], b_low[0])
    y_high[...], y_low[...] = halves(product(own, (m_high[...], m_low[...])))
    size = own[0].shape[1]
    s_own[...] = product((y_high[:, size : 2 * size], y_low[:, size : 2 * size]), own, True)


def kernel_side(which, sizes, inv, tile, b_high, b_low, s_in, y_high, y_low, s_out, m_high, m_low):
    read_inv(inv, tile, sizes, m_high, m_low)
    part = (b_high[which], b_low[which])
    y_high[...], y_low[...] = halves(product(part, (m_high[...], m_low[...])))
    size = part[0].shape[1]
    s_out[...] = s_in[...] + product((y_high[:, size : 2 * size], y_low[:, size : 2 * size]), part, True)


def kernel_next(sizes, y0_high, y0_low, y1_high, y1_low, y2_high, y2_low, div, s_next, n_high, n_low, p_high, p_low, dense):
    width, side = sizes[2], sizes[4]
    clear(dense)
    place_div(div_codes(integers(div), sizes), div, sizes, dense)
    size = n_high.shape[1]
    cut = slice(2 * size, 3 * size)
    for owner, (high, low) in enumerate(((y0_high, y0_low), (y1_high, y1_low), (y2_high, y2_low))):
        term = product((high[:, cut], low[:, cut]), owner_part(dense, owner, width), True)
        s_next[...] = term if owner == 0 else s_next[...] + term
        for u in range(width):
            block = slice(u * side, (u + 1) * side)
            p_high[owner * width + u], p_low[owner * width + u] = high[:, block], low[:, block]
    n_high[...], n_low[...] = owner_part(dense, 3, width)


def kernel_far(
    sizes, inv, tile, div, b_high, b_low, n_high, n_low, s_own, s_next, p_in_high, p_in_low, blocks, p_high, p_low, m_high, m_low
):
    rows, _, width, _, side = sizes
    read_inv(inv, tile, sizes, m_high, m_low)
    codes = target_codes(integers(div), rows, blocks.shape[1] + 1)
    own = (b_high[3], b_low[3])
    y_high, y_low = halves(product(own, (m_high[...], m_low[...])))
    size = own[0].shape[1]
    for u in range(width):
        cut = slice(u * side, (u + 1) * side)
        p_high[3 * width + u], p_low[3 * width + u] = y_high[:, cut], y_low[:, cut]
    cut = slice(size, 2 * size)
    own_sum = s_own[...] + product((y_high[:, cut], y_low[:, cut]), own, True)
    pick(blocks, own_sum, (0, 1), codes)
    cut = slice(2 * size, 3 * size)
    next_sum = s_next[...] + product((y_high[:, cut], y_low[:, cut]), (n_high[...], n_low[...]), True)
    pick(blocks, next_sum, (2,), codes)


def kernel_prev(sizes, div, own, p_high, p_low, blocks, out, buf, left_high, left_low, sems):
    rows, slots, _, _, side = sizes
    pattern = out.shape[1]
    copies = []
    for row in range(rows):
        copies.append(pltpu.make_async_copy(blocks.at[row], out.at[row, pl.ds(0, pattern - 1)], sems.at[0, row]))
        copies[-1].start()
    codes = div_codes(integers(div), sizes)
    targets = target_codes(integers(own), rows, pattern)
    for row in range(rows):
        target = targets[row * pattern + pattern - 1]
        place = pl.ds(row * side, side)
        other = jnp.maximum(target, 0)
        right = []
        for slot in range(slots):
            code = codes[slot]
            for i in range(1, rows):
                code = jnp.where(other == i, codes[i * slots + slot], code)
            cut = pl.ds(slot * side, side)
            source = pl.multiple_of((other * slots + slot) * side, side)
            live = jnp.where((code >= 0) & (target >= 0), 1.0, 0.0)
            right.append(div[pl.ds(source, side), :] * live)
            code = jnp.maximum(code, 0)
            left_high[:, cut], left_low[:, cut] = p_high[code, place, :], p_low[code, place, :]
        buf[row] = product((left_high[...], left_low[...]), halves(jnp.concatenate(right, axis=1)), True)
        copies.append(pltpu.make_async_copy(buf.at[row], out.at[row, pattern - 1], sems.at[1, row]))
        copies[-1].start()
    for copy in copies:
        copy.wait()


def kernel_all(sizes, d_meta, p_meta, n_meta, m_meta, s_meta, div, prev, follow, inv, out, dense, sums, m_high, m_low):
    _, _, width, slots, _ = sizes
    clear(dense)
    clear(sums)
    for region, (meta, blocks) in enumerate(((p_meta, prev), (d_meta, div), (n_meta, follow))):
        place_div(meta, blocks, sizes, dense.at[region])

    @pl.loop(0, inv.shape[0])
    def _(owner):
        clear(m_high)
        clear(m_low)
        codes = [m_meta[owner * width * slots + i] for i in range(width * slots)]
        place_inv(codes, inv.at[owner], sizes, m_high, m_low)
        size = m_high.shape[0]
        own = owner_part(dense.at[1], owner, width)
        y_high, y_low = halves(product(own, (m_high[...], m_low[...])))
        for region in range(3):
            cut = slice(region * size, (region + 1) * size)
            sums[region] += product((y_high[:, cut], y_low[:, cut]), owner_part(dense.at[region], owner, width), True)

    codes = [s_meta[i] for i in range(out.shape[0] * out.shape[1])]
    for slots, region in (((0, 1), 1), ((2,), 2), ((3,), 0)):
        pick(out, sums[region], slots, codes)


def call(kernel, operands, outs, scratch, flops, scalars=0, specs=None, out_specs=None, aliases=None, limit=24 << 20):
    moved = sum(x.size * x.dtype.itemsize for x in operands[scalars:] + outs)
    return pl.pallas_call(
        kernel,
        out_shape=outs if len(outs) > 1 else outs[0],
        in_specs=specs or [SMEM] * scalars + [VMEM] * (len(operands) - scalars),
        out_specs=out_specs or ([VMEM] * len(outs) if len(outs) > 1 else VMEM),
        scratch_shapes=scratch,
        input_output_aliases=aliases or {},
        compiler_params=pltpu.CompilerParams(vmem_limit_bytes=limit),
        cost_estimate=pl.CostEstimate(flops=flops, bytes_accessed=moved, transcendentals=0),
    )(*operands)


def local(div_blocks, div_owner, div_local, div_count, inv_blocks, inv_cols, inv_count, schur_cols, schur_count):
    rows, slots, side, _ = div_blocks.shape
    width, inv_slots = inv_cols.shape
    pattern = schur_cols.shape[1]
    owners = lax.axis_size("row")
    count = lax.axis_size("col")
    size, wide = width * side, 3 * width * side
    sizes = (rows, slots, width, inv_slots, side)
    forward = [(i, (i + 1) % count) for i in range(count)]
    backward = [(i, (i - 1) % count) for i in range(count)]
    div_flat = div_blocks.reshape(rows * slots * side, side)
    inv_flat = inv_blocks.reshape(width * inv_slots * side, side)

    square = jax.ShapeDtypeStruct((rows * side, rows * side), F32)
    half = jax.ShapeDtypeStruct((rows * side, size), BF16)
    every = jax.ShapeDtypeStruct((owners, rows * side, size), BF16)
    y_half = jax.ShapeDtypeStruct((rows * side, wide), BF16)
    result = jax.ShapeDtypeStruct((rows, pattern, side, side), F32)
    m_half = pltpu.VMEM((size, wide), BF16)
    one = 2 * 3 * rows * side * size * wide

    if owners != 4 or count % 2 or rows != 2 or side != 128 or pattern != 4:

        def order(length):
            return jnp.arange(length, dtype=jnp.int32)[None, :]

        d_meta = jnp.where(order(slots) < div_count[:, None], div_owner * width + div_local, -1).reshape(-1)
        m_meta = jnp.where(order(inv_slots) < inv_count[:, None], inv_cols, -1).reshape(-1)
        s_meta = jnp.where(order(pattern) < schur_count[:, None], schur_cols % rows, -1).reshape(-1)
        prev = lax.ppermute(div_flat, "col", forward)
        follow = lax.ppermute(div_flat, "col", backward)
        p_meta = lax.ppermute(d_meta, "col", forward)
        n_meta = lax.ppermute(d_meta, "col", backward)
        inv = lax.all_gather(inv_flat, "row")
        all_meta = lax.all_gather(m_meta, "row", tiled=True)
        return call(
            functools.partial(kernel_all, sizes),
            [d_meta, p_meta, n_meta, all_meta, s_meta, div_flat, prev, follow, inv],
            [result],
            [
                pltpu.VMEM((3, owners * width, rows * side, side), F32),
                pltpu.VMEM((3, rows * side, rows * side), F32),
                m_half,
                m_half,
            ],
            owners * one * 2,
            scalars=5,
            limit=56 << 20,
        )

    anywhere = pl.BlockSpec(memory_space=pl.ANY)

    def noted(blocks, tables):
        height = blocks.shape[0] + 8
        out, at = jnp.pad(blocks, ((0, 8), (0, 0))), blocks.shape[0]
        for table in tables:
            lines, length = table.shape
            out = out + jnp.pad(table.astype(F32), ((at, height - at - lines), (0, side - length)))
            at += lines
        return out

    inv_tables = (inv_cols, inv_count[None, :])
    div = lax.optimization_barrier(noted(div_flat, (div_owner, div_local)))
    div = lax.dynamic_update_slice(div, div_count[None, :].astype(F32), (div_flat.shape[0] + 2 * rows, 0))
    inv = noted(inv_flat, inv_tables)
    nothing = jnp.zeros((0, side), F32)
    tile = noted(nothing, inv_tables)
    pattern_tile = noted(nothing, (schur_cols, schur_count[None, :]))

    def swap(first):
        def partner(r, c):
            return r ^ (1 if (c % 2 == 0) == first else 2)

        return [(r * count + c, partner(r, c) * count + c) for r in range(owners) for c in range(count)]

    inv_1 = lax.ppermute(inv_flat, ("row", "col"), swap(True))
    inv_2 = lax.ppermute(inv, ("row", "col"), swap(False))
    follow = lax.ppermute(div, "col", backward)
    prev = lax.ppermute(div, "col", forward)

    m_scratch = [m_half, m_half]
    b_high, b_low, y0_high, y0_low, s_own = call(
        functools.partial(kernel_own, sizes),
        [div, inv],
        [every, every, y_half, y_half, square],
        [pltpu.VMEM((owners * width, rows * side, side), F32), *m_scratch],
        one * 4 // 3,
    )
    inv_1, s_own = lax.optimization_barrier((inv_1, s_own))
    inv_3 = lax.ppermute(inv_1, ("row", "col"), swap(False))
    tile_1 = lax.ppermute(tile, ("row", "col"), swap(True))
    tile_3 = lax.ppermute(tile_1, ("row", "col"), swap(False))
    y1_high, y1_low, s_own = call(
        functools.partial(kernel_side, 1, sizes), [inv_1, tile_1, b_high, b_low, s_own], [y_half, y_half, square], m_scratch, one * 4 // 3
    )
    y2_high, y2_low, s_own = call(
        functools.partial(kernel_side, 2, sizes), [inv_2, inv_2, b_high, b_low, s_own], [y_half, y_half, square], m_scratch, one * 4 // 3
    )
    p_half = jax.ShapeDtypeStruct((owners * width, rows * side, side), BF16)
    s_next, n_high, n_low, p_high, p_low = call(
        functools.partial(kernel_next, sizes),
        [y0_high, y0_low, y1_high, y1_low, y2_high, y2_low, follow],
        [square, half, half, p_half, p_half],
        [pltpu.VMEM((owners * width, rows * side, side), F32)],
        one,
    )
    three, p_high, p_low = call(
        functools.partial(kernel_far, sizes),
        [inv_3, tile_3, pattern_tile, b_high, b_low, n_high, n_low, s_own, s_next, p_high, p_low],
        [jax.ShapeDtypeStruct((rows, pattern - 1, side, side), F32), p_half, p_half],
        m_scratch,
        one * 5 // 3,
        aliases={9: 1, 10: 2},
    )
    left = pltpu.VMEM((side, slots * side), BF16)
    return call(
        functools.partial(kernel_prev, sizes),
        [prev, pattern_tile, p_high, p_low, three],
        [result],
        [pltpu.VMEM((rows, side, side), F32), left, left, pltpu.SemaphoreType.DMA((2, rows))],
        one,
        out_specs=anywhere,
    )


def solution(mesh):
    blocks = P(("row", "col"), None, None, None)
    table = P(("row", "col"), None)
    line = P(("row", "col"))
    return jax.shard_map(
        local,
        mesh=mesh,
        in_specs=(blocks, table, table, line, blocks, table, line, table, line),
        out_specs=blocks,
        check_vma=False,
    )
```

```python
import functools

import jax
import jax.numpy as jnp
from jax import lax
from jax.experimental import pallas as pl
from jax.experimental.pallas import tpu as pltpu
from jax.sharding import PartitionSpec as P

F32 = jnp.float32
BF16 = jnp.bfloat16
VMEM = pl.BlockSpec(memory_space=pltpu.VMEM)
SMEM = pl.BlockSpec(memory_space=pltpu.SMEM)
PACK_LIMIT = 60 << 20
PARTS = 4


def halves(value):
    high = value.astype(BF16)
    return high, (value - high.astype(F32)).astype(BF16)


def product(left, right, transposed=False):
    dims = (((1,), (1 if transposed else 0,)), ((), ()))
    dot = functools.partial(lax.dot_general, dimension_numbers=dims, preferred_element_type=F32)
    return dot(left[0], right[0]) + (dot(left[0], right[1]) + dot(left[1], right[0]))


def clear(ref):
    ref[...] = jnp.zeros(ref.shape, ref.dtype)


def place_div(codes, blocks, sizes, dense):
    rows, slots, _, _, side = sizes
    for row in range(rows):
        for slot in range(slots):
            code = codes[row * slots + slot]

            @pl.when(code >= 0)
            def _():
                dense[code, pl.ds(row * side, side), :] += blocks[pl.ds((row * slots + slot) * side, side), :]


def place_inv(codes, blocks, sizes, high, low):
    _, _, width, slots, side = sizes
    for row in range(width):
        for slot in range(slots):
            code = codes[row * slots + slot]

            @pl.when(code >= 0)
            def _():
                spot = (pl.ds(row * side, side), pl.ds(pl.multiple_of(code * side, side), side))
                high[spot], low[spot] = halves(blocks[pl.ds((row * slots + slot) * side, side), :])


def owner_part(dense, owner, width):
    return halves(jnp.concatenate([dense[owner * width + i] for i in range(width)], axis=1))


def pick(out, sums, slots, codes):
    rows, _, side, _ = out.shape
    pattern = len(codes) // rows
    for row in range(rows):
        for slot in slots:
            code = codes[row * pattern + slot]
            result = jnp.zeros((side, side), F32)
            for other in range(rows):
                block = sums[row * side : (row + 1) * side, other * side : (other + 1) * side]
                result = jnp.where(code == other, block, result)
            out[row, slot] = result


def fetch(sources, targets, sems):
    copies = [pltpu.make_async_copy(x, y, sems.at[i]) for i, (x, y) in enumerate(zip(sources, targets))]
    for copy in copies:
        copy.start()
    return copies


def kernel_pack(inv, div, *refs):
    tables, (inv_out, div_out, tile_out), scratch = refs[:7], refs[7:10], refs[10:]
    small_refs, (inv_buf, div_buf, small_sem, in_sem, out_sem) = scratch[:7], scratch[7:]
    small = fetch(tables, small_refs, small_sem)
    parts = in_sem.shape[1]
    arrays = ((inv, inv_buf, inv_out), (div, div_buf, div_out))
    cuts = [[pl.ds(j * (x.shape[0] // parts), x.shape[0] // parts) for j in range(parts)] for x in (inv, div)]
    reads, writes = [], []
    for i, (blocks, buf, out) in enumerate(arrays):
        reads += fetch([blocks.at[cut] for cut in cuts[i]], [buf.at[cut] for cut in cuts[i]], in_sem.at[i])
    for copy in small:
        copy.wait()
    for i, tables in enumerate((small_refs[:2], small_refs[2:])):
        _, buf, out = arrays[i]
        at = rows = buf.shape[0] - 8
        buf[pl.ds(rows, 8), :] = jnp.zeros((8, buf.shape[1]), F32)
        for table in tables:
            values = table[...].astype(F32)
            height, length = (1, *values.shape)[-2:]
            buf[pl.ds(at, height), pl.ds(0, length)] = values.reshape(height, length)
            at += height
        cuts[i].append(pl.ds(rows, 8))
    tile = pltpu.make_async_copy(inv_buf.at[cuts[0][-1]], tile_out, small_sem.at[0])
    tile.start()
    writes.append(tile)
    for i, (_, buf, out) in enumerate(arrays):
        for j, cut in enumerate(cuts[i]):
            if j < parts:
                reads[i * parts + j].wait()
            copy = pltpu.make_async_copy(buf.at[cut], out.at[cut], out_sem.at[i, j])
            copy.start()
            writes.append(copy)
    for copy in writes:
        copy.wait()


def integers(packed):
    return packed[pl.ds(packed.shape[0] - 8, 8), :].astype(jnp.int32)


def inv_codes(table, sizes):
    _, _, width, slots, _ = sizes
    codes = []
    for u in range(width):
        count = table[width, u]
        codes += [jnp.where(m < count, table[u, m], -1) for m in range(slots)]
    return codes


def div_codes(table, sizes):
    rows, slots, width, _, _ = sizes
    mine = lax.axis_index("row")
    odd = lax.axis_index("col") % 2
    codes = []
    for i in range(rows):
        count = table[2 * rows, i]
        for k in range(slots):
            apart = table[i, k] ^ mine
            apart = jnp.where(odd == 1, ((apart & 1) << 1) | (apart >> 1), apart)
            code = apart * width + table[rows + i, k]
            codes.append(jnp.where(k < count, code, -1))
    return codes


def target_codes(table, rows, pattern):
    codes = []
    for i in range(rows):
        count = table[rows, i]
        codes += [jnp.where(t < count, table[i, t] % rows, -1) for t in range(pattern)]
    return codes


def read_inv(inv, tile, sizes, m_high, m_low):
    clear(m_high)
    clear(m_low)
    place_inv(inv_codes(integers(tile), sizes), inv, sizes, m_high, m_low)


def kernel_own(sizes, div, inv, b_high, b_low, y_high, y_low, s_own, dense, m_high, m_low):
    clear(dense)
    read_inv(inv, inv, sizes, m_high, m_low)
    place_div(div_codes(integers(div), sizes), div, sizes, dense)
    for owner in range(b_high.shape[0]):
        b_high[owner], b_low[owner] = owner_part(dense, owner, sizes[2])
    own = (b_high[0], b_low[0])
    y_high[...], y_low[...] = halves(product(own, (m_high[...], m_low[...])))
    size = own[0].shape[1]
    s_own[...] = product((y_high[:, size : 2 * size], y_low[:, size : 2 * size]), own, True)


def kernel_side(which, sizes, inv, tile, b_high, b_low, s_in, y_high, y_low, s_out, m_high, m_low):
    read_inv(inv, tile, sizes, m_high, m_low)
    part = (b_high[which], b_low[which])
    y_high[...], y_low[...] = halves(product(part, (m_high[...], m_low[...])))
    size = part[0].shape[1]
    s_out[...] = s_in[...] + product((y_high[:, size : 2 * size], y_low[:, size : 2 * size]), part, True)


def kernel_next(sizes, y0_high, y0_low, y1_high, y1_low, y2_high, y2_low, div, s_next, n_high, n_low, p_high, p_low, dense):
    width, side = sizes[2], sizes[4]
    clear(dense)
    place_div(div_codes(integers(div), sizes), div, sizes, dense)
    size = n_high.shape[1]
    cut = slice(2 * size, 3 * size)
    for owner, (high, low) in enumerate(((y0_high, y0_low), (y1_high, y1_low), (y2_high, y2_low))):
        term = product((high[:, cut], low[:, cut]), owner_part(dense, owner, width), True)
        s_next[...] = term if owner == 0 else s_next[...] + term
        for u in range(width):
            block = slice(u * side, (u + 1) * side)
            p_high[owner * width + u], p_low[owner * width + u] = high[:, block], low[:, block]
    n_high[...], n_low[...] = owner_part(dense, 3, width)


def kernel_far(
    sizes, inv, tile, div, b_high, b_low, n_high, n_low, s_own, s_next, blocks, q_high, q_low, m_high, m_low
):
    rows, _, width, _, side = sizes
    read_inv(inv, tile, sizes, m_high, m_low)
    codes = target_codes(integers(div), rows, blocks.shape[1] + 1)
    own = (b_high[3], b_low[3])
    y_high, y_low = halves(product(own, (m_high[...], m_low[...])))
    size = own[0].shape[1]
    for u in range(width):
        cut = slice(u * side, (u + 1) * side)
        q_high[u], q_low[u] = y_high[:, cut], y_low[:, cut]
    cut = slice(size, 2 * size)
    own_sum = s_own[...] + product((y_high[:, cut], y_low[:, cut]), own, True)
    pick(blocks, own_sum, (0, 1), codes)
    cut = slice(2 * size, 3 * size)
    next_sum = s_next[...] + product((y_high[:, cut], y_low[:, cut]), (n_high[...], n_low[...]), True)
    pick(blocks, next_sum, (2,), codes)


def kernel_prev(sizes, div, own, p_high, p_low, q_high, q_low, blocks, out, buf, sems):
    rows, slots, _, _, side = sizes
    pattern = out.shape[1]
    known = p_high.shape[0]
    copies = []
    for row in range(rows):
        copies.append(pltpu.make_async_copy(blocks.at[row], out.at[row, pl.ds(0, pattern - 1)], sems.at[0, row]))
        copies[-1].start()
    codes = div_codes(integers(div), sizes)
    targets = target_codes(integers(own), rows, pattern)
    for row in range(rows):
        target = targets[row * pattern + pattern - 1]
        place = pl.ds(row * side, side)
        other = jnp.maximum(target, 0)
        left, right = ([], []), []
        for slot in range(slots):
            code = codes[slot]
            for i in range(1, rows):
                code = jnp.where(other == i, codes[i * slots + slot], code)
            source = pl.multiple_of((other * slots + slot) * side, side)
            live = jnp.where((code >= 0) & (target >= 0), 1.0, 0.0)
            right.append(div[pl.ds(source, side), :] * live)
            at, late = jnp.clip(code, 0, known - 1), jnp.maximum(code - known, 0)
            for part, early, last in zip(left, (p_high, p_low), (q_high, q_low)):
                part.append(jnp.where(code < known, early[at, place, :], last[late, place, :]))
        buf[row] = product([jnp.concatenate(x, axis=1) for x in left], halves(jnp.concatenate(right, axis=1)), True)
        copies.append(pltpu.make_async_copy(buf.at[row], out.at[row, pattern - 1], sems.at[1, row]))
        copies[-1].start()
    for copy in copies:
        copy.wait()


def kernel_all(sizes, d_meta, p_meta, n_meta, m_meta, s_meta, div, prev, follow, inv, out, dense, sums, m_high, m_low):
    _, _, width, slots, _ = sizes
    clear(dense)
    clear(sums)
    for region, (meta, blocks) in enumerate(((p_meta, prev), (d_meta, div), (n_meta, follow))):
        place_div(meta, blocks, sizes, dense.at[region])

    @pl.loop(0, inv.shape[0])
    def _(owner):
        clear(m_high)
        clear(m_low)
        codes = [m_meta[owner * width * slots + i] for i in range(width * slots)]
        place_inv(codes, inv.at[owner], sizes, m_high, m_low)
        size = m_high.shape[0]
        own = owner_part(dense.at[1], owner, width)
        y_high, y_low = halves(product(own, (m_high[...], m_low[...])))
        for region in range(3):
            cut = slice(region * size, (region + 1) * size)
            sums[region] += product((y_high[:, cut], y_low[:, cut]), owner_part(dense.at[region], owner, width), True)

    codes = [s_meta[i] for i in range(out.shape[0] * out.shape[1])]
    for slots, region in (((0, 1), 1), ((2,), 2), ((3,), 0)):
        pick(out, sums[region], slots, codes)


def call(kernel, operands, outs, scratch, flops, scalars=0, specs=None, out_specs=None, limit=24 << 20):
    moved = sum(x.size * x.dtype.itemsize for x in operands[scalars:] + outs)
    return pl.pallas_call(
        kernel,
        out_shape=outs if len(outs) > 1 else outs[0],
        in_specs=specs or [SMEM] * scalars + [VMEM] * (len(operands) - scalars),
        out_specs=out_specs or ([VMEM] * len(outs) if len(outs) > 1 else VMEM),
        scratch_shapes=scratch,
        compiler_params=pltpu.CompilerParams(vmem_limit_bytes=limit),
        cost_estimate=pl.CostEstimate(flops=flops, bytes_accessed=moved, transcendentals=0),
    )(*operands)


def local(div_blocks, div_owner, div_local, div_count, inv_blocks, inv_cols, inv_count, schur_cols, schur_count):
    rows, slots, side, _ = div_blocks.shape
    width, inv_slots = inv_cols.shape
    pattern = schur_cols.shape[1]
    owners = lax.axis_size("row")
    count = lax.axis_size("col")
    size, wide = width * side, 3 * width * side
    sizes = (rows, slots, width, inv_slots, side)
    forward = [(i, (i + 1) % count) for i in range(count)]
    backward = [(i, (i - 1) % count) for i in range(count)]
    div_flat = div_blocks.reshape(rows * slots * side, side)
    inv_flat = inv_blocks.reshape(width * inv_slots * side, side)

    square = jax.ShapeDtypeStruct((rows * side, rows * side), F32)
    half = jax.ShapeDtypeStruct((rows * side, size), BF16)
    every = jax.ShapeDtypeStruct((owners, rows * side, size), BF16)
    y_half = jax.ShapeDtypeStruct((rows * side, wide), BF16)
    result = jax.ShapeDtypeStruct((rows, pattern, side, side), F32)
    m_half = pltpu.VMEM((size, wide), BF16)
    one = 2 * 3 * rows * side * size * wide

    if owners != 4 or count % 2 or rows != 2 or side != 128 or pattern != 4:

        def order(length):
            return jnp.arange(length, dtype=jnp.int32)[None, :]

        d_meta = jnp.where(order(slots) < div_count[:, None], div_owner * width + div_local, -1).reshape(-1)
        m_meta = jnp.where(order(inv_slots) < inv_count[:, None], inv_cols, -1).reshape(-1)
        s_meta = jnp.where(order(pattern) < schur_count[:, None], schur_cols % rows, -1).reshape(-1)
        prev = lax.ppermute(div_flat, "col", forward)
        follow = lax.ppermute(div_flat, "col", backward)
        p_meta = lax.ppermute(d_meta, "col", forward)
        n_meta = lax.ppermute(d_meta, "col", backward)
        inv = lax.all_gather(inv_flat, "row")
        all_meta = lax.all_gather(m_meta, "row", tiled=True)
        return call(
            functools.partial(kernel_all, sizes),
            [d_meta, p_meta, n_meta, all_meta, s_meta, div_flat, prev, follow, inv],
            [result],
            [
                pltpu.VMEM((3, owners * width, rows * side, side), F32),
                pltpu.VMEM((3, rows * side, rows * side), F32),
                m_half,
                m_half,
            ],
            owners * one * 2,
            scalars=5,
            limit=56 << 20,
        )

    anywhere = pl.BlockSpec(memory_space=pl.ANY)

    def noted(blocks, tables):
        height = blocks.shape[0] + 8
        out, at = jnp.pad(blocks, ((0, 8), (0, 0))), blocks.shape[0]
        for table in tables:
            lines, length = table.shape
            out = out + jnp.pad(table.astype(F32), ((at, height - at - lines), (0, side - length)))
            at += lines
        return out

    inv_tables = (inv_cols, inv_count[None, :])
    div = lax.optimization_barrier(noted(div_flat, (div_owner, div_local)))
    div = lax.dynamic_update_slice(div, div_count[None, :].astype(F32), (div_flat.shape[0] + 2 * rows, 0))
    inv = noted(inv_flat, inv_tables)
    nothing = jnp.zeros((0, side), F32)
    tile = noted(nothing, inv_tables)
    pattern_tile = noted(nothing, (schur_cols, schur_count[None, :]))

    def swap(first):
        def partner(r, c):
            return r ^ (1 if (c % 2 == 0) == first else 2)

        return [(r * count + c, partner(r, c) * count + c) for r in range(owners) for c in range(count)]

    inv_1 = lax.ppermute(inv_flat, ("row", "col"), swap(True))
    inv_2 = lax.ppermute(inv, ("row", "col"), swap(False))
    follow = lax.ppermute(div, "col", backward)
    prev = lax.ppermute(div, "col", forward)

    m_scratch = [m_half, m_half]
    b_high, b_low, y0_high, y0_low, s_own = call(
        functools.partial(kernel_own, sizes),
        [div, inv],
        [every, every, y_half, y_half, square],
        [pltpu.VMEM((owners * width, rows * side, side), F32), *m_scratch],
        one * 4 // 3,
    )
    inv_1, s_own = lax.optimization_barrier((inv_1, s_own))
    inv_3 = lax.ppermute(inv_1, ("row", "col"), swap(False))
    tile_1 = lax.ppermute(tile, ("row", "col"), swap(True))
    tile_3 = lax.ppermute(tile_1, ("row", "col"), swap(False))
    y1_high, y1_low, s_own = call(
        functools.partial(kernel_side, 1, sizes), [inv_1, tile_1, b_high, b_low, s_own], [y_half, y_half, square], m_scratch, one * 4 // 3
    )
    y2_high, y2_low, s_own = call(
        functools.partial(kernel_side, 2, sizes), [inv_2, inv_2, b_high, b_low, s_own], [y_half, y_half, square], m_scratch, one * 4 // 3
    )
    p_half, q_half = (jax.ShapeDtypeStruct((n * width, rows * side, side), BF16) for n in (owners - 1, 1))
    s_next, n_high, n_low, p_high, p_low = call(
        functools.partial(kernel_next, sizes),
        [y0_high, y0_low, y1_high, y1_low, y2_high, y2_low, follow],
        [square, half, half, p_half, p_half],
        [pltpu.VMEM((owners * width, rows * side, side), F32)],
        one,
    )
    three, q_high, q_low = call(
        functools.partial(kernel_far, sizes),
        [inv_3, tile_3, pattern_tile, b_high, b_low, n_high, n_low, s_own, s_next],
        [jax.ShapeDtypeStruct((rows, pattern - 1, side, side), F32), q_half, q_half],
        m_scratch,
        one * 5 // 3,
    )
    return call(
        functools.partial(kernel_prev, sizes),
        [prev, pattern_tile, p_high, p_low, q_high, q_low, three],
        [result],
        [pltpu.VMEM((rows, side, side), F32), pltpu.SemaphoreType.DMA((2, rows))],
        one,
        out_specs=anywhere,
    )


def solution(mesh):
    blocks = P(("row", "col"), None, None, None)
    table = P(("row", "col"), None)
    line = P(("row", "col"))
    return jax.shard_map(
        local,
        mesh=mesh,
        in_specs=(blocks, table, table, line, blocks, table, line, table, line),
        out_specs=blocks,
        check_vma=False,
    )
```

```python
import functools

import jax
import jax.numpy as jnp
from jax import lax
from jax.experimental import pallas as pl
from jax.experimental.pallas import tpu as pltpu
from jax.sharding import PartitionSpec as P

F32 = jnp.float32
BF16 = jnp.bfloat16
VMEM = pl.BlockSpec(memory_space=pltpu.VMEM)
SMEM = pl.BlockSpec(memory_space=pltpu.SMEM)


def halves(value):
    high = value.astype(BF16)
    return high, (value - high.astype(F32)).astype(BF16)


def product(left, right, transposed=False):
    dims = (((1,), (1 if transposed else 0,)), ((), ()))
    dot = functools.partial(lax.dot_general, dimension_numbers=dims, preferred_element_type=F32)
    return dot(left[0], right[0]) + (dot(left[0], right[1]) + dot(left[1], right[0]))


def clear(ref):
    ref[...] = jnp.zeros(ref.shape, ref.dtype)


def place_div(codes, blocks, sizes, dense):
    rows, slots, _, _, side = sizes
    for row in range(rows):
        for slot in range(slots):
            code = codes[row * slots + slot]

            @pl.when(code >= 0)
            def _():
                dense[code, pl.ds(row * side, side), :] += blocks[pl.ds((row * slots + slot) * side, side), :]


def place_inv(codes, blocks, sizes, high, low):
    _, _, width, slots, side = sizes
    for row in range(width):
        for slot in range(slots):
            code = codes[row * slots + slot]

            @pl.when(code >= 0)
            def _():
                spot = (pl.ds(row * side, side), pl.ds(pl.multiple_of(code * side, side), side))
                high[spot], low[spot] = halves(blocks[pl.ds((row * slots + slot) * side, side), :])


def owner_part(dense, owner, width):
    return halves(jnp.concatenate([dense[owner * width + i] for i in range(width)], axis=1))


def pick(out, sums, slots, codes):
    rows, _, side, _ = out.shape
    pattern = len(codes) // rows
    for row in range(rows):
        for slot in slots:
            code = codes[row * pattern + slot]
            result = jnp.zeros((side, side), F32)
            for other in range(rows):
                block = sums[row * side : (row + 1) * side, other * side : (other + 1) * side]
                result = jnp.where(code == other, block, result)
            out[row, slot] = result


def integers(packed):
    return packed[pl.ds(packed.shape[0] - 8, 8), :].astype(jnp.int32)


def inv_codes(table, sizes):
    _, _, width, slots, _ = sizes
    codes = []
    for u in range(width):
        count = table[width, u]
        codes += [jnp.where(m < count, table[u, m], -1) for m in range(slots)]
    return codes


def div_codes(table, sizes):
    rows, slots, width, _, _ = sizes
    mine = lax.axis_index("row")
    odd = lax.axis_index("col") % 2
    codes = []
    for i in range(rows):
        count = table[2 * rows, i]
        for k in range(slots):
            apart = table[i, k] ^ mine
            apart = jnp.where(odd == 1, ((apart & 1) << 1) | (apart >> 1), apart)
            code = apart * width + table[rows + i, k]
            codes.append(jnp.where(k < count, code, -1))
    return codes


def target_codes(table, rows, pattern):
    codes = []
    for i in range(rows):
        count = table[rows, i]
        codes += [jnp.where(t < count, table[i, t] % rows, -1) for t in range(pattern)]
    return codes


def read_inv(inv, tile, sizes, m_high, m_low):
    clear(m_high)
    clear(m_low)
    place_inv(inv_codes(integers(tile), sizes), inv, sizes, m_high, m_low)


def kernel_own(sizes, div, inv, b_high, b_low, y_high, y_low, s_own, dense, m_high, m_low):
    clear(dense)
    read_inv(inv, inv, sizes, m_high, m_low)
    place_div(div_codes(integers(div), sizes), div, sizes, dense)
    for owner in range(b_high.shape[0]):
        b_high[owner], b_low[owner] = owner_part(dense, owner, sizes[2])
    own = (b_high[0], b_low[0])
    y_high[...], y_low[...] = halves(product(own, (m_high[...], m_low[...])))
    size = own[0].shape[1]
    s_own[...] = product((y_high[:, size : 2 * size], y_low[:, size : 2 * size]), own, True)


def kernel_side(which, sizes, inv, tile, b_high, b_low, s_in, y_high, y_low, s_out, m_high, m_low):
    read_inv(inv, tile, sizes, m_high, m_low)
    part = (b_high[which], b_low[which])
    y_high[...], y_low[...] = halves(product(part, (m_high[...], m_low[...])))
    size = part[0].shape[1]
    s_out[...] = s_in[...] + product((y_high[:, size : 2 * size], y_low[:, size : 2 * size]), part, True)


def kernel_next(sizes, y0_high, y0_low, y1_high, y1_low, y2_high, y2_low, div, s_next, n_high, n_low, p_high, p_low, dense):
    width, side = sizes[2], sizes[4]
    clear(dense)
    place_div(div_codes(integers(div), sizes), div, sizes, dense)
    size = n_high.shape[1]
    cut = slice(2 * size, 3 * size)
    for owner, (high, low) in enumerate(((y0_high, y0_low), (y1_high, y1_low), (y2_high, y2_low))):
        term = product((high[:, cut], low[:, cut]), owner_part(dense, owner, width), True)
        s_next[...] = term if owner == 0 else s_next[...] + term
        for u in range(width):
            block = slice(u * side, (u + 1) * side)
            p_high[owner * width + u], p_low[owner * width + u] = high[:, block], low[:, block]
    n_high[...], n_low[...] = owner_part(dense, 3, width)


def kernel_far(
    sizes, inv, tile, div, b_high, b_low, n_high, n_low, s_own, s_next, blocks, q_high, q_low, m_high, m_low
):
    rows, _, width, _, side = sizes
    read_inv(inv, tile, sizes, m_high, m_low)
    codes = target_codes(integers(div), rows, blocks.shape[1] + 1)
    own = (b_high[3], b_low[3])
    y_high, y_low = halves(product(own, (m_high[...], m_low[...])))
    size = own[0].shape[1]
    for u in range(width):
        cut = slice(u * side, (u + 1) * side)
        q_high[u], q_low[u] = y_high[:, cut], y_low[:, cut]
    cut = slice(size, 2 * size)
    own_sum = s_own[...] + product((y_high[:, cut], y_low[:, cut]), own, True)
    pick(blocks, own_sum, (0, 1), codes)
    cut = slice(2 * size, 3 * size)
    next_sum = s_next[...] + product((y_high[:, cut], y_low[:, cut]), (n_high[...], n_low[...]), True)
    pick(blocks, next_sum, (2,), codes)


def kernel_prev(sizes, div, own, p_high, p_low, q_high, q_low, blocks, out, buf, sems):
    rows, slots, _, _, side = sizes
    pattern = out.shape[1]
    known = p_high.shape[0]
    copies = []
    for row in range(rows):
        copies.append(pltpu.make_async_copy(blocks.at[row], out.at[row, pl.ds(0, pattern - 1)], sems.at[0, row]))
        copies[-1].start()
    codes = div_codes(integers(div), sizes)
    targets = target_codes(integers(own), rows, pattern)
    for row in range(rows):
        target = targets[row * pattern + pattern - 1]
        place = pl.ds(row * side, side)
        other = jnp.maximum(target, 0)
        left, right = ([], []), []
        for slot in range(slots):
            code = codes[slot]
            for i in range(1, rows):
                code = jnp.where(other == i, codes[i * slots + slot], code)
            source = pl.multiple_of((other * slots + slot) * side, side)
            live = jnp.where((code >= 0) & (target >= 0), 1.0, 0.0)
            right.append(div[pl.ds(source, side), :] * live)
            at, late = jnp.clip(code, 0, known - 1), jnp.maximum(code - known, 0)
            for part, early, last in zip(left, (p_high, p_low), (q_high, q_low)):
                part.append(jnp.where(code < known, early[at, place, :], last[late, place, :]))
        buf[row] = product([jnp.concatenate(x, axis=1) for x in left], halves(jnp.concatenate(right, axis=1)), True)
        copies.append(pltpu.make_async_copy(buf.at[row], out.at[row, pattern - 1], sems.at[1, row]))
        copies[-1].start()
    for copy in copies:
        copy.wait()


def kernel_all(sizes, d_meta, p_meta, n_meta, m_meta, s_meta, div, prev, follow, inv, out, dense, sums, m_high, m_low):
    _, _, width, slots, _ = sizes
    clear(dense)
    clear(sums)
    for region, (meta, blocks) in enumerate(((p_meta, prev), (d_meta, div), (n_meta, follow))):
        place_div(meta, blocks, sizes, dense.at[region])

    @pl.loop(0, inv.shape[0])
    def _(owner):
        clear(m_high)
        clear(m_low)
        codes = [m_meta[owner * width * slots + i] for i in range(width * slots)]
        place_inv(codes, inv.at[owner], sizes, m_high, m_low)
        size = m_high.shape[0]
        own = owner_part(dense.at[1], owner, width)
        y_high, y_low = halves(product(own, (m_high[...], m_low[...])))
        for region in range(3):
            cut = slice(region * size, (region + 1) * size)
            sums[region] += product((y_high[:, cut], y_low[:, cut]), owner_part(dense.at[region], owner, width), True)

    codes = [s_meta[i] for i in range(out.shape[0] * out.shape[1])]
    for slots, region in (((0, 1), 1), ((2,), 2), ((3,), 0)):
        pick(out, sums[region], slots, codes)


def call(kernel, operands, outs, scratch, flops, scalars=0, specs=None, out_specs=None, limit=24 << 20):
    moved = sum(x.size * x.dtype.itemsize for x in operands[scalars:] + outs)
    return pl.pallas_call(
        kernel,
        out_shape=outs if len(outs) > 1 else outs[0],
        in_specs=specs or [SMEM] * scalars + [VMEM] * (len(operands) - scalars),
        out_specs=out_specs or ([VMEM] * len(outs) if len(outs) > 1 else VMEM),
        scratch_shapes=scratch,
        compiler_params=pltpu.CompilerParams(vmem_limit_bytes=limit),
        cost_estimate=pl.CostEstimate(flops=flops, bytes_accessed=moved, transcendentals=0),
    )(*operands)


def local(div_blocks, div_owner, div_local, div_count, inv_blocks, inv_cols, inv_count, schur_cols, schur_count):
    rows, slots, side, _ = div_blocks.shape
    width, inv_slots = inv_cols.shape
    pattern = schur_cols.shape[1]
    owners = lax.axis_size("row")
    count = lax.axis_size("col")
    size, wide = width * side, 3 * width * side
    sizes = (rows, slots, width, inv_slots, side)
    forward = [(i, (i + 1) % count) for i in range(count)]
    backward = [(i, (i - 1) % count) for i in range(count)]
    div_flat = div_blocks.reshape(rows * slots * side, side)
    inv_flat = inv_blocks.reshape(width * inv_slots * side, side)

    square = jax.ShapeDtypeStruct((rows * side, rows * side), F32)
    half = jax.ShapeDtypeStruct((rows * side, size), BF16)
    every = jax.ShapeDtypeStruct((owners, rows * side, size), BF16)
    y_half = jax.ShapeDtypeStruct((rows * side, wide), BF16)
    result = jax.ShapeDtypeStruct((rows, pattern, side, side), F32)
    m_half = pltpu.VMEM((size, wide), BF16)
    one = 2 * 3 * rows * side * size * wide

    if owners != 4 or count % 2 or rows != 2 or side != 128 or pattern != 4:

        def order(length):
            return jnp.arange(length, dtype=jnp.int32)[None, :]

        d_meta = jnp.where(order(slots) < div_count[:, None], div_owner * width + div_local, -1).reshape(-1)
        m_meta = jnp.where(order(inv_slots) < inv_count[:, None], inv_cols, -1).reshape(-1)
        s_meta = jnp.where(order(pattern) < schur_count[:, None], schur_cols % rows, -1).reshape(-1)
        prev = lax.ppermute(div_flat, "col", forward)
        follow = lax.ppermute(div_flat, "col", backward)
        p_meta = lax.ppermute(d_meta, "col", forward)
        n_meta = lax.ppermute(d_meta, "col", backward)
        inv = lax.all_gather(inv_flat, "row")
        all_meta = lax.all_gather(m_meta, "row", tiled=True)
        return call(
            functools.partial(kernel_all, sizes),
            [d_meta, p_meta, n_meta, all_meta, s_meta, div_flat, prev, follow, inv],
            [result],
            [
                pltpu.VMEM((3, owners * width, rows * side, side), F32),
                pltpu.VMEM((3, rows * side, rows * side), F32),
                m_half,
                m_half,
            ],
            owners * one * 2,
            scalars=5,
            limit=56 << 20,
        )

    anywhere = pl.BlockSpec(memory_space=pl.ANY)

    def noted(blocks, tables):
        height = blocks.shape[0] + 8
        out, at = jnp.pad(blocks, ((0, 8), (0, 0))), blocks.shape[0]
        for table in tables:
            lines, length = table.shape
            out = out + jnp.pad(table.astype(F32), ((at, height - at - lines), (0, side - length)))
            at += lines
        return out

    inv_tables = (inv_cols, inv_count[None, :])
    div = lax.optimization_barrier(noted(div_flat, (div_owner, div_local)))
    div = lax.dynamic_update_slice(div, div_count[None, :].astype(F32), (div_flat.shape[0] + 2 * rows, 0))
    inv = noted(inv_flat, inv_tables)
    nothing = jnp.zeros((0, side), F32)
    tile = noted(nothing, inv_tables)
    pattern_tile = noted(nothing, (schur_cols, schur_count[None, :]))

    def swap(first):
        def partner(r, c):
            return r ^ (1 if (c % 2 == 0) == first else 2)

        return [(r * count + c, partner(r, c) * count + c) for r in range(owners) for c in range(count)]

    inv_1 = lax.ppermute(inv_flat, ("row", "col"), swap(True))
    inv_2 = lax.ppermute(inv, ("row", "col"), swap(False))
    follow = lax.ppermute(div, "col", backward)
    prev = lax.ppermute(div, "col", forward)

    m_scratch = [m_half, m_half]
    b_high, b_low, y0_high, y0_low, s_own = call(
        functools.partial(kernel_own, sizes),
        [div, inv],
        [every, every, y_half, y_half, square],
        [pltpu.VMEM((owners * width, rows * side, side), F32), *m_scratch],
        one * 4 // 3,
    )
    inv_1, s_own = lax.optimization_barrier((inv_1, s_own))
    inv_3 = lax.ppermute(inv_1, ("row", "col"), swap(False))
    tile_1 = lax.ppermute(tile, ("row", "col"), swap(True))
    tile_3 = lax.ppermute(tile_1, ("row", "col"), swap(False))
    y1_high, y1_low, s_own = call(
        functools.partial(kernel_side, 1, sizes), [inv_1, tile_1, b_high, b_low, s_own], [y_half, y_half, square], m_scratch, one * 4 // 3
    )
    y2_high, y2_low, s_own = call(
        functools.partial(kernel_side, 2, sizes), [inv_2, inv_2, b_high, b_low, s_own], [y_half, y_half, square], m_scratch, one * 4 // 3
    )
    p_half, q_half = (jax.ShapeDtypeStruct((n * width, rows * side, side), BF16) for n in (owners - 1, 1))
    s_next, n_high, n_low, p_high, p_low = call(
        functools.partial(kernel_next, sizes),
        [y0_high, y0_low, y1_high, y1_low, y2_high, y2_low, follow],
        [square, half, half, p_half, p_half],
        [pltpu.VMEM((owners * width, rows * side, side), F32)],
        one,
    )
    three, q_high, q_low = call(
        functools.partial(kernel_far, sizes),
        [inv_3, tile_3, pattern_tile, b_high, b_low, n_high, n_low, s_own, s_next],
        [jax.ShapeDtypeStruct((rows, pattern - 1, side, side), F32), q_half, q_half],
        m_scratch,
        one * 5 // 3,
    )
    return call(
        functools.partial(kernel_prev, sizes),
        [prev, pattern_tile, p_high, p_low, q_high, q_low, three],
        [result],
        [pltpu.VMEM((rows, side, side), F32), pltpu.SemaphoreType.DMA((2, rows))],
        one,
        out_specs=anywhere,
    )


def solution(mesh):
    blocks = P(("row", "col"), None, None, None)
    table = P(("row", "col"), None)
    line = P(("row", "col"))
    return jax.shard_map(
        local,
        mesh=mesh,
        in_specs=(blocks, table, table, line, blocks, table, line, table, line),
        out_specs=blocks,
        check_vma=False,
    )
```

```python
import functools

import jax
import jax.numpy as jnp
from jax import lax
from jax.experimental import pallas as pl
from jax.experimental.pallas import tpu as pltpu
from jax.sharding import PartitionSpec as P

F32 = jnp.float32
BF16 = jnp.bfloat16
VMEM = pl.BlockSpec(memory_space=pltpu.VMEM)
SMEM = pl.BlockSpec(memory_space=pltpu.SMEM)


def halves(value):
    high = value.astype(BF16)
    return high, (value - high.astype(F32)).astype(BF16)


def product(left, right, transposed=False):
    dims = (((1,), (1 if transposed else 0,)), ((), ()))
    dot = functools.partial(lax.dot_general, dimension_numbers=dims, preferred_element_type=F32)
    return dot(left[0], right[0]) + (dot(left[0], right[1]) + dot(left[1], right[0]))


def clear(ref):
    ref[...] = jnp.zeros(ref.shape, ref.dtype)


def place_div(codes, blocks, sizes, dense):
    rows, slots, _, _, side = sizes
    for row in range(rows):
        for slot in range(slots):
            code = codes[row * slots + slot]

            @pl.when(code >= 0)
            def _():
                dense[code, pl.ds(row * side, side), :] += blocks[pl.ds((row * slots + slot) * side, side), :]


def place_inv(codes, blocks, sizes, high, low):
    _, _, width, slots, side = sizes
    for row in range(width):
        for slot in range(slots):
            code = codes[row * slots + slot]

            @pl.when(code >= 0)
            def _():
                spot = (pl.ds(row * side, side), pl.ds(pl.multiple_of(code * side, side), side))
                high[spot], low[spot] = halves(blocks[pl.ds((row * slots + slot) * side, side), :])


def owner_part(dense, owner, width):
    return halves(jnp.concatenate([dense[owner * width + i] for i in range(width)], axis=1))


def pick(out, sums, slots, codes):
    rows, _, side, _ = out.shape
    pattern = len(codes) // rows
    for row in range(rows):
        for slot in slots:
            code = codes[row * pattern + slot]
            result = jnp.zeros((side, side), F32)
            for other in range(rows):
                block = sums[row * side : (row + 1) * side, other * side : (other + 1) * side]
                result = jnp.where(code == other, block, result)
            out[row, slot] = result


def integers(packed):
    return packed[pl.ds(packed.shape[0] - 8, 8), :].astype(jnp.int32)


def inv_codes(table, sizes):
    _, _, width, slots, _ = sizes
    codes = []
    for u in range(width):
        count = table[width, u]
        codes += [jnp.where(m < count, table[u, m], -1) for m in range(slots)]
    return codes


def div_codes(table, sizes):
    rows, slots, width, _, _ = sizes
    mine = lax.axis_index("row")
    odd = lax.axis_index("col") % 2
    codes = []
    for i in range(rows):
        count = table[2 * rows, i]
        for k in range(slots):
            apart = table[i, k] ^ mine
            apart = jnp.where(odd == 1, ((apart & 1) << 1) | (apart >> 1), apart)
            code = apart * width + table[rows + i, k]
            codes.append(jnp.where(k < count, code, -1))
    return codes


def target_codes(table, rows, pattern):
    codes = []
    for i in range(rows):
        count = table[rows, i]
        codes += [jnp.where(t < count, table[i, t] % rows, -1) for t in range(pattern)]
    return codes


def read_inv(inv, tile, sizes, m_high, m_low):
    clear(m_high)
    clear(m_low)
    place_inv(inv_codes(integers(tile), sizes), inv, sizes, m_high, m_low)


def kernel_own(sizes, div, inv, b_high, b_low, y_high, y_low, s_own, dense, m_high, m_low):
    clear(dense)
    read_inv(inv, inv, sizes, m_high, m_low)
    place_div(div_codes(integers(div), sizes), div, sizes, dense)
    for owner in range(b_high.shape[0]):
        b_high[owner], b_low[owner] = owner_part(dense, owner, sizes[2])
    own = (b_high[0], b_low[0])
    y_high[...], y_low[...] = halves(product(own, (m_high[...], m_low[...])))
    size = own[0].shape[1]
    s_own[...] = product((y_high[:, size : 2 * size], y_low[:, size : 2 * size]), own, True)


def kernel_side(which, sizes, inv, tile, b_high, b_low, s_in, y_high, y_low, s_out, m_high, m_low):
    read_inv(inv, tile, sizes, m_high, m_low)
    part = (b_high[which], b_low[which])
    y_high[...], y_low[...] = halves(product(part, (m_high[...], m_low[...])))
    size = part[0].shape[1]
    s_out[...] = s_in[...] + product((y_high[:, size : 2 * size], y_low[:, size : 2 * size]), part, True)


def kernel_next(sizes, y0_high, y0_low, y1_high, y1_low, y2_high, y2_low, div, s_next, n_high, n_low, p_high, p_low, dense):
    width, side = sizes[2], sizes[4]
    clear(dense)
    place_div(div_codes(integers(div), sizes), div, sizes, dense)
    size = n_high.shape[1]
    cut = slice(2 * size, 3 * size)
    for owner, (high, low) in enumerate(((y0_high, y0_low), (y1_high, y1_low), (y2_high, y2_low))):
        term = product((high[:, cut], low[:, cut]), owner_part(dense, owner, width), True)
        s_next[...] = term if owner == 0 else s_next[...] + term
        for u in range(width):
            block = slice(u * side, (u + 1) * side)
            p_high[owner * width + u], p_low[owner * width + u] = high[:, block], low[:, block]
    n_high[...], n_low[...] = owner_part(dense, 3, width)


def kernel_far(
    sizes, inv, tile, div, b_high, b_low, n_high, n_low, s_own, s_next, blocks, q_high, q_low, m_high, m_low
):
    rows, _, width, _, side = sizes
    read_inv(inv, tile, sizes, m_high, m_low)
    codes = target_codes(integers(div), rows, blocks.shape[1] + 1)
    own = (b_high[3], b_low[3])
    y_high, y_low = halves(product(own, (m_high[...], m_low[...])))
    size = own[0].shape[1]
    for u in range(width):
        cut = slice(u * side, (u + 1) * side)
        q_high[u], q_low[u] = y_high[:, cut], y_low[:, cut]
    cut = slice(size, 2 * size)
    own_sum = s_own[...] + product((y_high[:, cut], y_low[:, cut]), own, True)
    pick(blocks, own_sum, (0, 1), codes)
    cut = slice(2 * size, 3 * size)
    next_sum = s_next[...] + product((y_high[:, cut], y_low[:, cut]), (n_high[...], n_low[...]), True)
    pick(blocks, next_sum, (2,), codes)


def kernel_prev(sizes, div, own, p_high, p_low, q_high, q_low, blocks, out, buf, sems):
    rows, slots, _, _, side = sizes
    pattern = out.shape[1]
    known = p_high.shape[0]
    copies = []
    for row in range(rows):
        copies.append(pltpu.make_async_copy(blocks.at[row], out.at[row, pl.ds(0, pattern - 1)], sems.at[0, row]))
        copies[-1].start()
    codes = div_codes(integers(div), sizes)
    targets = target_codes(integers(own), rows, pattern)
    factors = []
    for row in range(rows):
        target = targets[row * pattern + pattern - 1]
        place = pl.ds(row * side, side)
        other = jnp.maximum(target, 0)
        left, right = ([], []), []
        for slot in range(slots):
            code = codes[slot]
            for i in range(1, rows):
                code = jnp.where(other == i, codes[i * slots + slot], code)
            source = pl.multiple_of((other * slots + slot) * side, side)
            live = jnp.where((code >= 0) & (target >= 0), 1.0, 0.0)
            right.append(halves(div[pl.ds(source, side), :] * live))
            at, late = jnp.clip(code, 0, known - 1), jnp.maximum(code - known, 0)
            for part, early, last in zip(left, (p_high, p_low), (q_high, q_low)):
                part.append(jnp.where(code < known, early[at, place, :], last[late, place, :]))
        factors.append([[jnp.concatenate(x, axis=1) for x in pair] for pair in (left, zip(*right))])
    for row, (left, right) in enumerate(factors):
        buf[row] = product(left, right, True)
        copies.append(pltpu.make_async_copy(buf.at[row], out.at[row, pattern - 1], sems.at[1, row]))
        copies[-1].start()
    for copy in copies:
        copy.wait()


def kernel_all(sizes, d_meta, p_meta, n_meta, m_meta, s_meta, div, prev, follow, inv, out, dense, sums, m_high, m_low):
    _, _, width, slots, _ = sizes
    clear(dense)
    clear(sums)
    for region, (meta, blocks) in enumerate(((p_meta, prev), (d_meta, div), (n_meta, follow))):
        place_div(meta, blocks, sizes, dense.at[region])

    @pl.loop(0, inv.shape[0])
    def _(owner):
        clear(m_high)
        clear(m_low)
        codes = [m_meta[owner * width * slots + i] for i in range(width * slots)]
        place_inv(codes, inv.at[owner], sizes, m_high, m_low)
        size = m_high.shape[0]
        own = owner_part(dense.at[1], owner, width)
        y_high, y_low = halves(product(own, (m_high[...], m_low[...])))
        for region in range(3):
            cut = slice(region * size, (region + 1) * size)
            sums[region] += product((y_high[:, cut], y_low[:, cut]), owner_part(dense.at[region], owner, width), True)

    codes = [s_meta[i] for i in range(out.shape[0] * out.shape[1])]
    for slots, region in (((0, 1), 1), ((2,), 2), ((3,), 0)):
        pick(out, sums[region], slots, codes)


def call(kernel, operands, outs, scratch, flops, scalars=0, specs=None, out_specs=None, limit=24 << 20):
    moved = sum(x.size * x.dtype.itemsize for x in operands[scalars:] + outs)
    return pl.pallas_call(
        kernel,
        out_shape=outs if len(outs) > 1 else outs[0],
        in_specs=specs or [SMEM] * scalars + [VMEM] * (len(operands) - scalars),
        out_specs=out_specs or ([VMEM] * len(outs) if len(outs) > 1 else VMEM),
        scratch_shapes=scratch,
        compiler_params=pltpu.CompilerParams(vmem_limit_bytes=limit),
        cost_estimate=pl.CostEstimate(flops=flops, bytes_accessed=moved, transcendentals=0),
    )(*operands)


def local(div_blocks, div_owner, div_local, div_count, inv_blocks, inv_cols, inv_count, schur_cols, schur_count):
    rows, slots, side, _ = div_blocks.shape
    width, inv_slots = inv_cols.shape
    pattern = schur_cols.shape[1]
    owners = lax.axis_size("row")
    count = lax.axis_size("col")
    size, wide = width * side, 3 * width * side
    sizes = (rows, slots, width, inv_slots, side)
    forward = [(i, (i + 1) % count) for i in range(count)]
    backward = [(i, (i - 1) % count) for i in range(count)]
    div_flat = div_blocks.reshape(rows * slots * side, side)
    inv_flat = inv_blocks.reshape(width * inv_slots * side, side)

    square = jax.ShapeDtypeStruct((rows * side, rows * side), F32)
    half = jax.ShapeDtypeStruct((rows * side, size), BF16)
    every = jax.ShapeDtypeStruct((owners, rows * side, size), BF16)
    y_half = jax.ShapeDtypeStruct((rows * side, wide), BF16)
    result = jax.ShapeDtypeStruct((rows, pattern, side, side), F32)
    m_half = pltpu.VMEM((size, wide), BF16)
    one = 2 * 3 * rows * side * size * wide

    if owners != 4 or count % 2 or rows != 2 or side != 128 or pattern != 4:

        def order(length):
            return jnp.arange(length, dtype=jnp.int32)[None, :]

        d_meta = jnp.where(order(slots) < div_count[:, None], div_owner * width + div_local, -1).reshape(-1)
        m_meta = jnp.where(order(inv_slots) < inv_count[:, None], inv_cols, -1).reshape(-1)
        s_meta = jnp.where(order(pattern) < schur_count[:, None], schur_cols % rows, -1).reshape(-1)
        prev = lax.ppermute(div_flat, "col", forward)
        follow = lax.ppermute(div_flat, "col", backward)
        p_meta = lax.ppermute(d_meta, "col", forward)
        n_meta = lax.ppermute(d_meta, "col", backward)
        inv = lax.all_gather(inv_flat, "row")
        all_meta = lax.all_gather(m_meta, "row", tiled=True)
        return call(
            functools.partial(kernel_all, sizes),
            [d_meta, p_meta, n_meta, all_meta, s_meta, div_flat, prev, follow, inv],
            [result],
            [
                pltpu.VMEM((3, owners * width, rows * side, side), F32),
                pltpu.VMEM((3, rows * side, rows * side), F32),
                m_half,
                m_half,
            ],
            owners * one * 2,
            scalars=5,
            limit=56 << 20,
        )

    anywhere = pl.BlockSpec(memory_space=pl.ANY)

    def noted(blocks, tables):
        height = blocks.shape[0] + 8
        out, at = jnp.pad(blocks, ((0, 8), (0, 0))), blocks.shape[0]
        for table in tables:
            lines, length = table.shape
            out = out + jnp.pad(table.astype(F32), ((at, height - at - lines), (0, side - length)))
            at += lines
        return out

    inv_tables = (inv_cols, inv_count[None, :])
    div = lax.optimization_barrier(noted(div_flat, (div_owner, div_local)))
    div = lax.dynamic_update_slice(div, div_count[None, :].astype(F32), (div_flat.shape[0] + 2 * rows, 0))
    inv = noted(inv_flat, inv_tables)
    nothing = jnp.zeros((0, side), F32)
    tile = noted(nothing, inv_tables)
    pattern_tile = noted(nothing, (schur_cols, schur_count[None, :]))

    def swap(first):
        def partner(r, c):
            return r ^ (1 if (c % 2 == 0) == first else 2)

        return [(r * count + c, partner(r, c) * count + c) for r in range(owners) for c in range(count)]

    inv_1 = lax.ppermute(inv_flat, ("row", "col"), swap(True))
    inv_2 = lax.ppermute(inv, ("row", "col"), swap(False))
    follow = lax.ppermute(div, "col", backward)
    prev = lax.ppermute(div, "col", forward)

    m_scratch = [m_half, m_half]
    b_high, b_low, y0_high, y0_low, s_own = call(
        functools.partial(kernel_own, sizes),
        [div, inv],
        [every, every, y_half, y_half, square],
        [pltpu.VMEM((owners * width, rows * side, side), F32), *m_scratch],
        one * 4 // 3,
    )
    inv_1, s_own = lax.optimization_barrier((inv_1, s_own))
    inv_3 = lax.ppermute(inv_1, ("row", "col"), swap(False))
    tile_1 = lax.ppermute(tile, ("row", "col"), swap(True))
    tile_3 = lax.ppermute(tile_1, ("row", "col"), swap(False))
    y1_high, y1_low, s_own = call(
        functools.partial(kernel_side, 1, sizes), [inv_1, tile_1, b_high, b_low, s_own], [y_half, y_half, square], m_scratch, one * 4 // 3
    )
    y2_high, y2_low, s_own = call(
        functools.partial(kernel_side, 2, sizes), [inv_2, inv_2, b_high, b_low, s_own], [y_half, y_half, square], m_scratch, one * 4 // 3
    )
    p_half, q_half = (jax.ShapeDtypeStruct((n * width, rows * side, side), BF16) for n in (owners - 1, 1))
    s_next, n_high, n_low, p_high, p_low = call(
        functools.partial(kernel_next, sizes),
        [y0_high, y0_low, y1_high, y1_low, y2_high, y2_low, follow],
        [square, half, half, p_half, p_half],
        [pltpu.VMEM((owners * width, rows * side, side), F32)],
        one,
    )
    three, q_high, q_low = call(
        functools.partial(kernel_far, sizes),
        [inv_3, tile_3, pattern_tile, b_high, b_low, n_high, n_low, s_own, s_next],
        [jax.ShapeDtypeStruct((rows, pattern - 1, side, side), F32), q_half, q_half],
        m_scratch,
        one * 5 // 3,
    )
    return call(
        functools.partial(kernel_prev, sizes),
        [prev, pattern_tile, p_high, p_low, q_high, q_low, three],
        [result],
        [pltpu.VMEM((rows, side, side), F32), pltpu.SemaphoreType.DMA((2, rows))],
        one,
        out_specs=anywhere,
    )


def solution(mesh):
    blocks = P(("row", "col"), None, None, None)
    table = P(("row", "col"), None)
    line = P(("row", "col"))
    return jax.shard_map(
        local,
        mesh=mesh,
        in_specs=(blocks, table, table, line, blocks, table, line, table, line),
        out_specs=blocks,
        check_vma=False,
    )
```

```python
import functools

import jax
import jax.numpy as jnp
from jax import lax
from jax.experimental import pallas as pl
from jax.experimental.pallas import tpu as pltpu
from jax.sharding import PartitionSpec as P

F32 = jnp.float32
BF16 = jnp.bfloat16
VMEM = pl.BlockSpec(memory_space=pltpu.VMEM)
SMEM = pl.BlockSpec(memory_space=pltpu.SMEM)
PACK_LIMIT = 60 << 20
PARTS = 4


def halves(value):
    high = value.astype(BF16)
    return high, (value - high.astype(F32)).astype(BF16)


def product(left, right, transposed=False):
    dims = (((1,), (1 if transposed else 0,)), ((), ()))
    dot = functools.partial(lax.dot_general, dimension_numbers=dims, preferred_element_type=F32)
    return dot(left[0], right[0]) + (dot(left[0], right[1]) + dot(left[1], right[0]))


def clear(ref):
    ref[...] = jnp.zeros(ref.shape, ref.dtype)


def place_div(codes, blocks, sizes, dense):
    rows, slots, _, _, side = sizes
    for row in range(rows):
        for slot in range(slots):
            code = codes[row * slots + slot]

            @pl.when(code >= 0)
            def _():
                dense[code, pl.ds(row * side, side), :] += blocks[pl.ds((row * slots + slot) * side, side), :]


def place_inv(codes, blocks, sizes, high, low):
    _, _, width, slots, side = sizes
    for row in range(width):
        for slot in range(slots):
            code = codes[row * slots + slot]

            @pl.when(code >= 0)
            def _():
                spot = (pl.ds(row * side, side), pl.ds(pl.multiple_of(code * side, side), side))
                high[spot], low[spot] = halves(blocks[pl.ds((row * slots + slot) * side, side), :])


def owner_part(dense, owner, width):
    return halves(jnp.concatenate([dense[owner * width + i] for i in range(width)], axis=1))


def pick(out, sums, slots, codes):
    rows, _, side, _ = out.shape
    pattern = len(codes) // rows
    for row in range(rows):
        for slot in slots:
            code = codes[row * pattern + slot]
            result = jnp.zeros((side, side), F32)
            for other in range(rows):
                block = sums[row * side : (row + 1) * side, other * side : (other + 1) * side]
                result = jnp.where(code == other, block, result)
            out[row, slot] = result


def fetch(sources, targets, sems):
    copies = [pltpu.make_async_copy(x, y, sems.at[i]) for i, (x, y) in enumerate(zip(sources, targets))]
    for copy in copies:
        copy.start()
    return copies


def kernel_pack(inv, div, *refs):
    tables, (inv_out, div_out, tile_out), scratch = refs[:7], refs[7:10], refs[10:]
    small_refs, (inv_buf, div_buf, small_sem, in_sem, out_sem) = scratch[:7], scratch[7:]
    small = fetch(tables, small_refs, small_sem)
    parts = in_sem.shape[1]
    arrays = ((inv, inv_buf, inv_out), (div, div_buf, div_out))
    cuts = [[pl.ds(j * (x.shape[0] // parts), x.shape[0] // parts) for j in range(parts)] for x in (inv, div)]
    reads, writes = [], []
    for i, (blocks, buf, out) in enumerate(arrays):
        reads += fetch([blocks.at[cut] for cut in cuts[i]], [buf.at[cut] for cut in cuts[i]], in_sem.at[i])
    for copy in small:
        copy.wait()
    for i, tables in enumerate((small_refs[:2], small_refs[2:])):
        _, buf, out = arrays[i]
        at = rows = buf.shape[0] - 8
        buf[pl.ds(rows, 8), :] = jnp.zeros((8, buf.shape[1]), F32)
        for table in tables:
            values = table[...].astype(F32)
            height, length = (1, *values.shape)[-2:]
            buf[pl.ds(at, height), pl.ds(0, length)] = values.reshape(height, length)
            at += height
        cuts[i].append(pl.ds(rows, 8))
    tile = pltpu.make_async_copy(inv_buf.at[cuts[0][-1]], tile_out, small_sem.at[0])
    tile.start()
    writes.append(tile)
    for i, (_, buf, out) in enumerate(arrays):
        for j, cut in enumerate(cuts[i]):
            if j < parts:
                reads[i * parts + j].wait()
            copy = pltpu.make_async_copy(buf.at[cut], out.at[cut], out_sem.at[i, j])
            copy.start()
            writes.append(copy)
    for copy in writes:
        copy.wait()


def integers(packed):
    return packed[pl.ds(packed.shape[0] - 8, 8), :].astype(jnp.int32)


def inv_codes(table, sizes):
    _, _, width, slots, _ = sizes
    codes = []
    for u in range(width):
        count = table[width, u]
        codes += [jnp.where(m < count, table[u, m], -1) for m in range(slots)]
    return codes


def div_codes(table, sizes):
    rows, slots, width, _, _ = sizes
    mine = lax.axis_index("row")
    odd = lax.axis_index("col") % 2
    codes = []
    for i in range(rows):
        count = table[2 * rows, i]
        for k in range(slots):
            apart = table[i, k] ^ mine
            apart = jnp.where(odd == 1, ((apart & 1) << 1) | (apart >> 1), apart)
            code = apart * width + table[rows + i, k]
            codes.append(jnp.where(k < count, code, -1))
    return codes


def target_codes(table, rows, pattern):
    codes = []
    for i in range(rows):
        count = table[rows, i]
        codes += [jnp.where(t < count, table[i, t] % rows, -1) for t in range(pattern)]
    return codes


def read_inv(inv, tile, sizes, m_high, m_low):
    clear(m_high)
    clear(m_low)
    place_inv(inv_codes(integers(tile), sizes), inv, sizes, m_high, m_low)


def kernel_own(sizes, div, inv, b_high, b_low, y_high, y_low, s_own, dense, m_high, m_low):
    clear(dense)
    read_inv(inv, inv, sizes, m_high, m_low)
    place_div(div_codes(integers(div), sizes), div, sizes, dense)
    for owner in range(b_high.shape[0]):
        b_high[owner], b_low[owner] = owner_part(dense, owner, sizes[2])
    own = (b_high[0], b_low[0])
    y_high[...], y_low[...] = halves(product(own, (m_high[...], m_low[...])))
    size = own[0].shape[1]
    s_own[...] = product((y_high[:, size : 2 * size], y_low[:, size : 2 * size]), own, True)


def kernel_side(which, sizes, inv, tile, b_high, b_low, s_in, y_high, y_low, s_out, m_high, m_low):
    read_inv(inv, tile, sizes, m_high, m_low)
    part = (b_high[which], b_low[which])
    y_high[...], y_low[...] = halves(product(part, (m_high[...], m_low[...])))
    size = part[0].shape[1]
    s_out[...] = s_in[...] + product((y_high[:, size : 2 * size], y_low[:, size : 2 * size]), part, True)


def kernel_next(sizes, y0_high, y0_low, y1_high, y1_low, y2_high, y2_low, div, s_next, n_high, n_low, p_high, p_low, dense):
    width, side = sizes[2], sizes[4]
    clear(dense)
    place_div(div_codes(integers(div), sizes), div, sizes, dense)
    size = n_high.shape[1]
    cut = slice(2 * size, 3 * size)
    for owner, (high, low) in enumerate(((y0_high, y0_low), (y1_high, y1_low), (y2_high, y2_low))):
        term = product((high[:, cut], low[:, cut]), owner_part(dense, owner, width), True)
        s_next[...] = term if owner == 0 else s_next[...] + term
        for u in range(width):
            block = slice(u * side, (u + 1) * side)
            p_high[owner * width + u], p_low[owner * width + u] = high[:, block], low[:, block]
    n_high[...], n_low[...] = owner_part(dense, 3, width)


def kernel_far(
    sizes, inv, tile, div, b_high, b_low, n_high, n_low, s_own, s_next, blocks, q_high, q_low, m_high, m_low
):
    rows, _, width, _, side = sizes
    read_inv(inv, tile, sizes, m_high, m_low)
    codes = target_codes(integers(div), rows, blocks.shape[1] + 1)
    own = (b_high[3], b_low[3])
    y_high, y_low = halves(product(own, (m_high[...], m_low[...])))
    size = own[0].shape[1]
    for u in range(width):
        cut = slice(u * side, (u + 1) * side)
        q_high[u], q_low[u] = y_high[:, cut], y_low[:, cut]
    cut = slice(size, 2 * size)
    own_sum = s_own[...] + product((y_high[:, cut], y_low[:, cut]), own, True)
    pick(blocks, own_sum, (0, 1), codes)
    cut = slice(2 * size, 3 * size)
    next_sum = s_next[...] + product((y_high[:, cut], y_low[:, cut]), (n_high[...], n_low[...]), True)
    pick(blocks, next_sum, (2,), codes)


def kernel_prev(sizes, div, own, p_high, p_low, q_high, q_low, blocks, out, buf, sems):
    rows, slots, _, _, side = sizes
    pattern = out.shape[1]
    known = p_high.shape[0]
    copies = []
    for row in range(rows):
        copies.append(pltpu.make_async_copy(blocks.at[row], out.at[row, pl.ds(0, pattern - 1)], sems.at[0, row]))
        copies[-1].start()
    codes = div_codes(integers(div), sizes)
    targets = target_codes(integers(own), rows, pattern)
    for row in range(rows):
        target = targets[row * pattern + pattern - 1]
        place = pl.ds(row * side, side)
        other = jnp.maximum(target, 0)
        left, right = ([], []), []
        for slot in range(slots):
            code = codes[slot]
            for i in range(1, rows):
                code = jnp.where(other == i, codes[i * slots + slot], code)
            source = pl.multiple_of((other * slots + slot) * side, side)
            live = jnp.where((code >= 0) & (target >= 0), 1.0, 0.0)
            right.append(div[pl.ds(source, side), :] * live)
            at, late = jnp.clip(code, 0, known - 1), jnp.maximum(code - known, 0)
            for part, early, last in zip(left, (p_high, p_low), (q_high, q_low)):
                part.append(jnp.where(code < known, early[at, place, :], last[late, place, :]))
        buf[row] = product([jnp.concatenate(x, axis=1) for x in left], halves(jnp.concatenate(right, axis=1)), True)
        copies.append(pltpu.make_async_copy(buf.at[row], out.at[row, pattern - 1], sems.at[1, row]))
        copies[-1].start()
    for copy in copies:
        copy.wait()


def kernel_all(sizes, d_meta, p_meta, n_meta, m_meta, s_meta, div, prev, follow, inv, out, dense, sums, m_high, m_low):
    _, _, width, slots, _ = sizes
    clear(dense)
    clear(sums)
    for region, (meta, blocks) in enumerate(((p_meta, prev), (d_meta, div), (n_meta, follow))):
        place_div(meta, blocks, sizes, dense.at[region])

    @pl.loop(0, inv.shape[0])
    def _(owner):
        clear(m_high)
        clear(m_low)
        codes = [m_meta[owner * width * slots + i] for i in range(width * slots)]
        place_inv(codes, inv.at[owner], sizes, m_high, m_low)
        size = m_high.shape[0]
        own = owner_part(dense.at[1], owner, width)
        y_high, y_low = halves(product(own, (m_high[...], m_low[...])))
        for region in range(3):
            cut = slice(region * size, (region + 1) * size)
            sums[region] += product((y_high[:, cut], y_low[:, cut]), owner_part(dense.at[region], owner, width), True)

    codes = [s_meta[i] for i in range(out.shape[0] * out.shape[1])]
    for slots, region in (((0, 1), 1), ((2,), 2), ((3,), 0)):
        pick(out, sums[region], slots, codes)


def call(kernel, operands, outs, scratch, flops, scalars=0, specs=None, out_specs=None, limit=24 << 20):
    moved = sum(x.size * x.dtype.itemsize for x in operands[scalars:] + outs)
    return pl.pallas_call(
        kernel,
        out_shape=outs if len(outs) > 1 else outs[0],
        in_specs=specs or [SMEM] * scalars + [VMEM] * (len(operands) - scalars),
        out_specs=out_specs or ([VMEM] * len(outs) if len(outs) > 1 else VMEM),
        scratch_shapes=scratch,
        compiler_params=pltpu.CompilerParams(vmem_limit_bytes=limit),
        cost_estimate=pl.CostEstimate(flops=flops, bytes_accessed=moved, transcendentals=0),
    )(*operands)


def local(div_blocks, div_owner, div_local, div_count, inv_blocks, inv_cols, inv_count, schur_cols, schur_count):
    rows, slots, side, _ = div_blocks.shape
    width, inv_slots = inv_cols.shape
    pattern = schur_cols.shape[1]
    owners = lax.axis_size("row")
    count = lax.axis_size("col")
    size, wide = width * side, 3 * width * side
    sizes = (rows, slots, width, inv_slots, side)
    forward = [(i, (i + 1) % count) for i in range(count)]
    backward = [(i, (i - 1) % count) for i in range(count)]
    div_flat = div_blocks.reshape(rows * slots * side, side)
    inv_flat = inv_blocks.reshape(width * inv_slots * side, side)

    square = jax.ShapeDtypeStruct((rows * side, rows * side), F32)
    half = jax.ShapeDtypeStruct((rows * side, size), BF16)
    every = jax.ShapeDtypeStruct((owners, rows * side, size), BF16)
    y_half = jax.ShapeDtypeStruct((rows * side, wide), BF16)
    result = jax.ShapeDtypeStruct((rows, pattern, side, side), F32)
    m_half = pltpu.VMEM((size, wide), BF16)
    one = 2 * 3 * rows * side * size * wide

    if owners != 4 or count % 2 or rows != 2 or side != 128 or pattern != 4:

        def order(length):
            return jnp.arange(length, dtype=jnp.int32)[None, :]

        d_meta = jnp.where(order(slots) < div_count[:, None], div_owner * width + div_local, -1).reshape(-1)
        m_meta = jnp.where(order(inv_slots) < inv_count[:, None], inv_cols, -1).reshape(-1)
        s_meta = jnp.where(order(pattern) < schur_count[:, None], schur_cols % rows, -1).reshape(-1)
        prev = lax.ppermute(div_flat, "col", forward)
        follow = lax.ppermute(div_flat, "col", backward)
        p_meta = lax.ppermute(d_meta, "col", forward)
        n_meta = lax.ppermute(d_meta, "col", backward)
        inv = lax.all_gather(inv_flat, "row")
        all_meta = lax.all_gather(m_meta, "row", tiled=True)
        return call(
            functools.partial(kernel_all, sizes),
            [d_meta, p_meta, n_meta, all_meta, s_meta, div_flat, prev, follow, inv],
            [result],
            [
                pltpu.VMEM((3, owners * width, rows * side, side), F32),
                pltpu.VMEM((3, rows * side, rows * side), F32),
                m_half,
                m_half,
            ],
            owners * one * 2,
            scalars=5,
            limit=56 << 20,
        )

    anywhere = pl.BlockSpec(memory_space=pl.ANY)

    def noted(blocks, tables):
        height = blocks.shape[0] + 8
        out, at = jnp.pad(blocks, ((0, 8), (0, 0))), blocks.shape[0]
        for table in tables:
            lines, length = table.shape
            out = out + jnp.pad(table.astype(F32), ((at, height - at - lines), (0, side - length)))
            at += lines
        return out

    inv_tables = (inv_cols, inv_count[None, :])
    div = lax.optimization_barrier(noted(div_flat, (div_owner, div_local)))
    div = lax.dynamic_update_slice(div, div_count[None, :].astype(F32), (div_flat.shape[0] + 2 * rows, 0))
    inv = noted(inv_flat, inv_tables)
    nothing = jnp.zeros((0, side), F32)
    tile = noted(nothing, inv_tables)
    pattern_tile = noted(nothing, (schur_cols, schur_count[None, :]))

    def swap(first):
        def partner(r, c):
            return r ^ (1 if (c % 2 == 0) == first else 2)

        return [(r * count + c, partner(r, c) * count + c) for r in range(owners) for c in range(count)]

    inv_1 = lax.ppermute(inv_flat, ("row", "col"), swap(True))
    inv_2 = lax.ppermute(inv, ("row", "col"), swap(False))
    follow = lax.ppermute(div, "col", backward)
    prev = lax.ppermute(div, "col", forward)

    m_scratch = [m_half, m_half]
    b_high, b_low, y0_high, y0_low, s_own = call(
        functools.partial(kernel_own, sizes),
        [div, inv],
        [every, every, y_half, y_half, square],
        [pltpu.VMEM((owners * width, rows * side, side), F32), *m_scratch],
        one * 4 // 3,
    )
    inv_3 = lax.ppermute(inv_1, ("row", "col"), swap(False))
    tile_1 = lax.ppermute(tile, ("row", "col"), swap(True))
    tile_3 = lax.ppermute(tile_1, ("row", "col"), swap(False))
    y1_high, y1_low, s_own = call(
        functools.partial(kernel_side, 1, sizes), [inv_1, tile_1, b_high, b_low, s_own], [y_half, y_half, square], m_scratch, one * 4 // 3
    )
    y2_high, y2_low, s_own = call(
        functools.partial(kernel_side, 2, sizes), [inv_2, inv_2, b_high, b_low, s_own], [y_half, y_half, square], m_scratch, one * 4 // 3
    )
    p_half, q_half = (jax.ShapeDtypeStruct((n * width, rows * side, side), BF16) for n in (owners - 1, 1))
    s_next, n_high, n_low, p_high, p_low = call(
        functools.partial(kernel_next, sizes),
        [y0_high, y0_low, y1_high, y1_low, y2_high, y2_low, follow],
        [square, half, half, p_half, p_half],
        [pltpu.VMEM((owners * width, rows * side, side), F32)],
        one,
    )
    three, q_high, q_low = call(
        functools.partial(kernel_far, sizes),
        [inv_3, tile_3, pattern_tile, b_high, b_low, n_high, n_low, s_own, s_next],
        [jax.ShapeDtypeStruct((rows, pattern - 1, side, side), F32), q_half, q_half],
        m_scratch,
        one * 5 // 3,
    )
    return call(
        functools.partial(kernel_prev, sizes),
        [prev, pattern_tile, p_high, p_low, q_high, q_low, three],
        [result],
        [pltpu.VMEM((rows, side, side), F32), pltpu.SemaphoreType.DMA((2, rows))],
        one,
        out_specs=anywhere,
    )


def solution(mesh):
    blocks = P(("row", "col"), None, None, None)
    table = P(("row", "col"), None)
    line = P(("row", "col"))
    return jax.shard_map(
        local,
        mesh=mesh,
        in_specs=(blocks, table, table, line, blocks, table, line, table, line),
        out_specs=blocks,
        check_vma=False,
    )
```
